256 devices in a mesh: docs: 32 (over x, z), vocab: 8 (over y, core).
Axes of the slice: x: 4, y: 4, z: 8, core: 2. Of those that a mesh axis runs over, the one named last changes fastest.
Arguments:
- tokens: bfloat16 [512, 80, 128], P(('docs', 'vocab')), may hold values from -6 to 6
- token_mask: int32 [512, 80], P(('docs', 'vocab')), may hold values from 0 to 1, as said below
- adapter_weight: bfloat16 [128, 768], replicated, may hold values from -0.5 to 0.5
- norm_gain: float32 [768], replicated, may hold values from 0.1 to 1.9
- head_weight: bfloat16 [768, 30720], P(None, 'vocab'), may hold values from -0.21875 to 0.21875
- head_bias: float32 [30720], P('vocab'), may hold values from -8 to 8
- block_counts: int32 [8, 32], P('vocab'), may hold values from 0 to 2, as said below
Outputs:
- postings: float32 [64, 512, 1024], P('docs', None, 'vocab')
The draws below stay inside these ranges and needn't reach their ends.
Inputs may be any that keep to these rules, and one draw needn't show every extreme that they name: `token_mask`: each passage's live slots are a prefix of at least 16 slots; the first passage of every run of 16 passages is full. `block_counts`: each row sums to 30, and in each row one owner has exactly 2.
All inputs are finite; a program needn't handle non-finite values.
Results may differ from the reference program's by a relative error of at most 0.0012.
Values may be sent and summed in bfloat16 or wider, within the bound.
A program may use at most 128 MiB of HBM per device.

```python
import jax
import jax.numpy as jnp
from jax import lax

CDIM = 128
HID = 768
BLOCK = 128
LEN = 80
NB = 30
OWN_CAP = 2
PASS_GRP = 16
PASSAGES = 512
VOCAB = 30720
N_DOCS = 32
N_VOCAB = 8


def counts_row(row_key):
    key_pick, key_big = jax.random.split(row_key)
    slot_total = (N_DOCS - 1) * OWN_CAP
    order = jax.random.permutation(key_pick, slot_total)
    chosen = (order < NB - OWN_CAP).astype(jnp.int32)
    per_owner = chosen.reshape(N_DOCS - 1, OWN_CAP).sum(axis=1).astype(jnp.int32)
    big_owner = jax.random.randint(key_big, (), 0, N_DOCS)
    owner_ids = jnp.arange(N_DOCS, dtype=jnp.int32)
    source_ids = jnp.clip(owner_ids - (owner_ids > big_owner).astype(jnp.int32), 0, N_DOCS - 2)
    return jnp.where(owner_ids == big_owner, OWN_CAP, per_owner[source_ids]).astype(jnp.int32)


def draw_block_counts(key, part):
    row_keys = jax.random.split(jax.random.fold_in(key, 11), N_VOCAB)
    return jax.vmap(counts_row)(row_keys)


def draw_token_mask(key, part):
    shortest = min(16, LEN // 2)
    lengths = jax.random.randint(jax.random.fold_in(key, 23), (PASSAGES,), shortest, LEN + 1)
    passage_ids = jnp.arange(PASSAGES, dtype=jnp.int32)
    lengths = jnp.where(passage_ids % PASS_GRP == 0, LEN, lengths)
    return (jnp.arange(LEN, dtype=jnp.int32)[None, :] < lengths[:, None]).astype(jnp.int32)


def block_levels(own_key, shape, pieces, low, top_value):
    def one(axis_at, shards_of):
        draws = jax.random.uniform(jax.random.fold_in(jax.random.fold_in(own_key, 6), axis_at), (shards_of,), jnp.float32, low / len(pieces), top_value / len(pieces))
        return jnp.repeat(jnp.exp(draws), shape[axis_at] // shards_of).reshape((-1,) + (1,) * (len(shape) - axis_at - 1))

    loudness = one(*pieces[0])
    for cut in pieces[1:]:
        loudness = loudness * one(*cut)
    return loudness


def gaussian(rng, extent, deviation, reach, cuts=(), kind=jnp.bfloat16):
    drawn = deviation * jax.random.normal(rng, extent, jnp.float32)
    if cuts:
        drawn = drawn * block_levels(rng, extent, cuts, -0.22, 0.18)
    return jnp.clip(drawn, -reach, reach).astype(kind)


def setup_inputs(seed: int = 0) -> dict:
    key_list = jax.random.split(jax.random.key(seed), 8)
    tokens = gaussian(key_list[0], (PASSAGES, LEN, CDIM), 1.0, 6.0, ((0, 256),))
    token_mask = draw_token_mask(jax.random.fold_in(key_list[7], 71), 0)
    adapter_weight = gaussian(key_list[2], (CDIM, HID), CDIM ** -0.5, 0.5)
    norm_gain = jnp.clip(1.0 + 0.18 * jax.random.normal(key_list[3], (HID,), jnp.float32), 0.1, 1.9)
    head_weight = gaussian(key_list[4], (HID, VOCAB), HID ** -0.5, 0.21875, ((1, 8),))
    head_bias = gaussian(key_list[5], (VOCAB,), 2.0, 8.0, ((0, 8),), jnp.float32)
    block_counts = draw_block_counts(jax.random.fold_in(key_list[7], 71), 0)
    return dict(tokens=tokens, token_mask=token_mask, adapter_weight=adapter_weight, norm_gain=norm_gain, head_weight=head_weight, head_bias=head_bias, block_counts=block_counts)


EPSILON = 1e-05

def layer_norm(adapted, norm_gain):
    row_mean = lax.optimization_barrier(jnp.mean(adapted, axis=-1, keepdims=True))
    centred = adapted - row_mean
    row_var = lax.optimization_barrier(jnp.mean(centred * centred, axis=-1, keepdims=True))
    return (centred * lax.rsqrt(row_var + EPSILON) * norm_gain).astype(jnp.bfloat16)

def reference(tokens, token_mask, adapter_weight, norm_gain, head_weight, head_bias, block_counts):

    def group_pool(inputs):
        group_tokens, group_mask = inputs
        adapted = jnp.dot(group_tokens.reshape(-1, CDIM), adapter_weight, preferred_element_type=jnp.float32)
        hidden = layer_norm(adapted, norm_gain)
        logits = jnp.dot(hidden, head_weight, preferred_element_type=jnp.float32) + head_bias
        impact = jnp.log1p(jnp.maximum(logits, 0.0)).reshape(PASS_GRP, LEN, VOCAB)
        return lax.optimization_barrier(jnp.max(impact * group_mask.astype(jnp.float32)[:, :, None], axis=1))
    grouped = (tokens.reshape(N_DOCS, PASS_GRP, LEN, CDIM), token_mask.reshape(N_DOCS, PASS_GRP, LEN))
    pooled = lax.map(group_pool, grouped).reshape(PASSAGES, VOCAB)
    term_peak = lax.optimization_barrier(jnp.max(pooled, axis=0))
    scaled = pooled / jnp.maximum(term_peak, 1.0)
    starts = jnp.cumsum(block_counts, axis=1).astype(jnp.int32) - block_counts
    slot_ids = jnp.arange(OWN_CAP, dtype=jnp.int32)
    block_index = jnp.clip(starts[:, :, None] + slot_ids[None, None, :], 0, NB - 1).astype(jnp.int32)
    is_live = (slot_ids[None, None, :] < block_counts[:, :, None]).astype(jnp.float32)
    blocks = scaled.reshape(PASSAGES, N_VOCAB, NB, BLOCK)
    shard_ids = jnp.arange(N_VOCAB, dtype=jnp.int32)[:, None, None]
    picked = blocks[:, shard_ids, block_index, :]
    picked = picked * is_live[None, :, :, :, None]
    return jnp.transpose(picked, (2, 3, 0, 1, 4)).reshape(N_DOCS * OWN_CAP, PASSAGES, N_VOCAB * BLOCK)
```

```python
import functools

import jax
import jax.numpy as jnp
from jax import lax
from jax.experimental import pallas as pl
from jax.experimental.pallas import tpu as pltpu
from jax.sharding import PartitionSpec as P

MESH = pl.DeviceIdType.MESH
BLOCK = 128
EPSILON = 1e-05
OWNERS = 32
CHIPS_Y = 4
NB = 30
LEN = 80
HALF = 8 * LEN
SHARD = 2 * LEN
TILE = 768
STEPS = NB * BLOCK // TILE
PIECE = HALF // STEPS


def index_kernel(
    tok_ref, mask_ref, aw_ref, gain_ref, bias_ref, counts_ref, hw_hbm, recv_ref,
    gtok, hid, wbuf, pooled, send, starts, wsem, tok_send, tok_recv, tile_send, tile_recv, tile_own,
):
    d = lax.axis_index("docs")
    v = lax.axis_index("vocab")
    y = v // 2
    c = v % 2
    y1 = y + 1 - 2 * (y % 2)
    y2 = (y + 2) % CHIPS_Y
    y3 = CHIPS_Y - 1 - y
    pair = y // 2
    near = [y1 * 2 + c, y1 * 2 + 1 - c, y * 2 + 1 - c]
    far = [y3 * 2 + c, y2 * 2 + c, y3 * 2 + 1 - c, y2 * 2 + 1 - c]

    def weight_copy(i):
        cols = pl.ds(pl.multiple_of(i * TILE, BLOCK), TILE)
        return pltpu.make_async_copy(hw_hbm.at[:, cols], wbuf.at[i], wsem.at[i])

    for i in range(STEPS):
        weight_copy(i).start()

    barrier = pltpu.get_barrier_semaphore()
    for partner in near + far:
        pl.semaphore_signal(barrier, inc=1, device_id=(d, partner), device_id_type=MESH)

    def greet(t, carry):
        pl.semaphore_signal(
            barrier, inc=1, device_id=((d + t) % OWNERS, v), device_id_type=MESH
        )
        return carry

    lax.fori_loop(1, OWNERS, greet, 0)

    slot = lax.broadcasted_iota(jnp.int32, (LEN, BLOCK), 0).astype(jnp.float32)
    mine = pl.multiple_of(v * SHARD, 16)
    for p in range(2):
        live = jnp.sum(mask_ref[p : p + 1, :].astype(jnp.float32), axis=1, keepdims=True)
        tok = tok_ref[p].astype(jnp.float32)
        tok = jnp.where(slot < live, tok, tok[0:1, :])
        gtok[pl.ds(pl.multiple_of(mine + p * LEN, 16), LEN), :] = tok.astype(jnp.bfloat16)

    def note_start(o, at):
        starts[o] = jnp.minimum(at, NB - 1)
        return at + counts_ref[0, o]

    lax.fori_loop(0, OWNERS, note_start, jnp.int32(0))

    pl.semaphore_wait(barrier, OWNERS - 1 + 7)

    def token_copy(r, partner, owner):
        rows = pl.ds(pl.multiple_of(owner * SHARD, 16), SHARD)
        return pltpu.make_async_remote_copy(
            src_ref=gtok.at[rows],
            dst_ref=gtok.at[rows],
            send_sem=tok_send.at[r],
            recv_sem=tok_recv.at[r],
            device_id=(d, partner),
            device_id_type=MESH,
        )

    for r, partner in enumerate(near + far):
        token_copy(r, partner, v).start()

    def norm_rows(src, dst):
        adapted = jnp.dot(
            gtok[pl.ds(pl.multiple_of(src, 16), PIECE), :], aw_ref[...], preferred_element_type=jnp.float32
        )
        centred = adapted - jnp.mean(adapted, axis=-1, keepdims=True)
        row_var = jnp.mean(centred * centred, axis=-1, keepdims=True)
        normed = centred * lax.rsqrt(row_var + EPSILON) * gain_ref[...]
        hid[pl.ds(pl.multiple_of(dst, 16), PIECE), :] = normed.astype(jnp.bfloat16)

    def head_step(k, i):
        logits = jnp.dot(hid[k * HALF : (k + 1) * HALF, :], wbuf[i], preferred_element_type=jnp.float32)
        x = jnp.maximum(jnp.max(logits.reshape(8, LEN, TILE), axis=1) + bias_ref[i], 0.0)
        for _ in range(3):
            x = x * (x + 2.0)
        for q in range(TILE // BLOCK):
            pooled[k, i * (TILE // BLOCK) + q] = x[:, q * BLOCK : (q + 1) * BLOCK]

    def tiles_of(k, o):
        at = starts[o]
        two = jnp.concatenate(
            [pooled[k, at], pooled[k, jnp.minimum(at + 1, NB - 1)]], axis=0
        )
        send[k, o] = two.astype(jnp.bfloat16)

    def send_tiles(k, half):
        def one(t, carry):
            o = (d + t) % OWNERS
            tiles_of(k, o)
            pltpu.make_async_remote_copy(
                src_ref=send.at[k, o],
                dst_ref=recv_ref.at[half, d],
                send_sem=tile_send.at[k],
                recv_sem=tile_recv.at[k],
                device_id=(o, v),
                device_id_type=MESH,
            ).start()
            return carry

        lax.fori_loop(1, OWNERS, one, 0)
        tiles_of(k, d)
        pltpu.make_async_copy(send.at[k, d], recv_ref.at[half, d], tile_own.at[k]).start()

    for r, partner in enumerate(near):
        token_copy(r, v, partner).wait_recv()
    for r, partner in enumerate(far):
        token_copy(r + 3, v, partner).wait_recv()
    for i in range(STEPS):
        weight_copy(i).wait()
    first = pair * HALF

    def norm_first(i, carry):
        norm_rows(first + i * PIECE, i * PIECE)
        return carry

    lax.fori_loop(0, STEPS, norm_first, 0)
    second = (1 - pair) * HALF

    def head_first(i, carry):
        head_step(0, i)
        norm_rows(second + i * PIECE, HALF + i * PIECE)
        return carry

    lax.fori_loop(0, STEPS, head_first, 0)
    send_tiles(0, pair)

    def head_second(i, carry):
        head_step(1, i)
        return carry

    lax.fori_loop(0, STEPS, head_second, 0)
    send_tiles(1, 1 - pair)

    for r, partner in enumerate(near + far):
        token_copy(r, partner, v).wait_send()
    for k, half in enumerate((pair, 1 - pair)):
        pltpu.make_async_copy(send.at[k, d], recv_ref.at[half, d], tile_own.at[k]).wait()
        others = send.at[k, 0 : OWNERS - 1]
        pltpu.make_async_copy(others, others, tile_send.at[k]).wait()
        others = recv_ref.at[half, 0 : OWNERS - 1]
        pltpu.make_async_copy(others, others, tile_recv.at[k]).wait()


def scale_kernel(counts_ref, code_ref, out_ref):
    owner = lax.axis_index("docs")
    count = counts_ref[0, owner]
    for s in range(2):
        code = code_ref[:, :, s * 8 : (s + 1) * 8, :].astype(jnp.float32)
        top = jnp.max(code.reshape(-1, 8, BLOCK), axis=0)
        top = jnp.max(top, axis=0, keepdims=True)
        peak = jnp.maximum(jnp.log1p(top) * 0.125, 1.0)
        factor = jnp.where(s < count, 0.125 / peak, 0.0)
        for h in range(2):
            out_ref[s, :, h] = jnp.log1p(code[h]) * factor


def shards(tokens, token_mask, adapter_weight, norm_gain, head_weight, head_bias, block_counts):
    vmem = pl.BlockSpec(memory_space=pltpu.VMEM)
    smem = pl.BlockSpec(memory_space=pltpu.SMEM)
    hbm = pl.BlockSpec(memory_space=pl.ANY)
    codes = pl.pallas_call(
        index_kernel,
        out_shape=jax.ShapeDtypeStruct((2, OWNERS, 16, BLOCK), jnp.bfloat16),
        in_specs=[vmem, vmem, vmem, vmem, vmem, smem, hbm],
        out_specs=hbm,
        scratch_shapes=[
            pltpu.VMEM((2 * HALF, BLOCK), jnp.bfloat16),
            pltpu.VMEM((2 * HALF, 768), jnp.bfloat16),
            pltpu.VMEM((STEPS, 768, TILE), jnp.bfloat16),
            pltpu.VMEM((2, NB, 8, BLOCK), jnp.float32),
            pltpu.VMEM((2, OWNERS, 16, BLOCK), jnp.bfloat16),
            pltpu.SMEM((OWNERS,), jnp.int32),
            pltpu.SemaphoreType.DMA((STEPS,)),
            pltpu.SemaphoreType.DMA((7,)),
            pltpu.SemaphoreType.DMA((7,)),
            pltpu.SemaphoreType.DMA((2,)),
            pltpu.SemaphoreType.DMA((2,)),
            pltpu.SemaphoreType.DMA((2,)),
        ],
        compiler_params=pltpu.CompilerParams(
            collective_id=0, has_side_effects=True, vmem_limit_bytes=48 * 2**20
        ),
        cost_estimate=pl.CostEstimate(
            flops=8_000_000_000, bytes_accessed=7_000_000, transcendentals=0
        ),
        name="index",
    )(
        tokens,
        token_mask,
        adapter_weight,
        norm_gain.reshape(1, -1),
        head_bias.reshape(STEPS, 1, TILE),
        block_counts,
        head_weight,
    )
    scaled = pl.pallas_call(
        scale_kernel,
        out_shape=jax.ShapeDtypeStruct((2, OWNERS, 2, 8, BLOCK), jnp.float32),
        in_specs=[smem, vmem],
        out_specs=vmem,
        compiler_params=pltpu.CompilerParams(vmem_limit_bytes=8 * 2**20),
        cost_estimate=pl.CostEstimate(flops=4_000_000, bytes_accessed=800_000, transcendentals=131072),
        name="scale",
    )(block_counts, codes)
    return scaled.reshape(2, OWNERS * 16, BLOCK)


def solution(mesh):
    in_specs = (
        P(("docs", "vocab"), None, None),
        P(("docs", "vocab"), None),
        P(),
        P(),
        P(None, "vocab"),
        P("vocab"),
        P("vocab", None),
    )
    out_specs = P("docs", None, "vocab")
    return jax.shard_map(shards, mesh=mesh, in_specs=in_specs, out_specs=out_specs, check_vma=False)
```

```python
import functools

import jax
import jax.numpy as jnp
from jax import lax
from jax.experimental import pallas as pl
from jax.experimental.pallas import tpu as pltpu
from jax.sharding import PartitionSpec as P

MESH = pl.DeviceIdType.MESH
BLOCK = 128
EPSILON = 1e-05
OWNERS = 32
CHIPS_Y = 4
NB = 30
LEN = 80
HALF = 8 * LEN
SHARD = 2 * LEN
TILE = 768
STEPS = NB * BLOCK // TILE
PIECE = HALF // STEPS


def index_kernel(
    tok_hbm, mask_hbm, aw_hbm, gain_hbm, bias_hbm, counts_hbm, hw_hbm, recv_ref,
    tok_ref, mask_ref, aw_ref, gain_ref, bias_ref, counts_ref,
    near_tok, far_tok, hid, wbuf, pooled, send, starts,
    arg_sem, wsem, tok_send, tok_recv, tile_send, tile_recv, tile_own,
):
    d = lax.axis_index("docs")
    v = lax.axis_index("vocab")
    y = v // 2
    c = v % 2
    y1 = y + 1 - 2 * (y % 2)
    y2 = (y + 2) % CHIPS_Y
    y3 = CHIPS_Y - 1 - y
    pair = y // 2
    near = [y1 * 2 + c, y1 * 2 + 1 - c, y * 2 + 1 - c]
    far = [y3 * 2 + c, y2 * 2 + c, y3 * 2 + 1 - c, y2 * 2 + 1 - c]

    arg_copies = [
        pltpu.make_async_copy(src, dst, arg_sem.at[i])
        for i, (src, dst) in enumerate((
            (tok_hbm, tok_ref), (mask_hbm, mask_ref), (aw_hbm, aw_ref),
            (gain_hbm, gain_ref), (bias_hbm, bias_ref), (counts_hbm, counts_ref),
        ))
    ]
    for copy in arg_copies:
        copy.start()

    def weight_copy(i):
        cols = slice(i * TILE, (i + 1) * TILE)
        return pltpu.make_async_copy(hw_hbm.at[:, cols], wbuf.at[i], wsem.at[i])

    for i in range(STEPS):
        weight_copy(i).start()

    barrier = pltpu.get_barrier_semaphore()
    for partner in near + far:
        pl.semaphore_signal(barrier, inc=1, device_id=(d, partner), device_id_type=MESH)

    def greet(t, carry):
        pl.semaphore_signal(
            barrier, inc=1, device_id=((d + t) % OWNERS, v), device_id_type=MESH
        )
        return carry

    lax.fori_loop(1, OWNERS, greet, 0)

    slot = lax.broadcasted_iota(jnp.int32, (LEN, BLOCK), 0).astype(jnp.float32)
    arg_copies[0].wait()
    arg_copies[1].wait()
    for p in range(2):
        live = jnp.sum(mask_ref[p : p + 1, :].astype(jnp.float32), axis=1, keepdims=True)
        tok = tok_ref[p].astype(jnp.float32)
        tok = jnp.where(slot < live, tok, tok[0:1, :])
        near_tok[v % 4, p * LEN : (p + 1) * LEN, :] = tok.astype(jnp.bfloat16)

    pl.semaphore_wait(barrier, OWNERS - 1 + 7)

    def token_copy(r, partner, owner):
        return pltpu.make_async_remote_copy(
            src_ref=near_tok.at[owner % 4],
            dst_ref=(near_tok if r < 3 else far_tok).at[owner % 4],
            send_sem=tok_send.at[r],
            recv_sem=tok_recv.at[r],
            device_id=(d, partner),
            device_id_type=MESH,
        )

    for r, partner in enumerate(near + far):
        token_copy(r, partner, v).start()

    arg_copies[5].wait()

    def note_start(o, at):
        starts[o] = jnp.minimum(at, NB - 1)
        return at + counts_ref[0, o]

    lax.fori_loop(0, OWNERS, note_start, jnp.int32(0))
    for i in (2, 3, 4):
        arg_copies[i].wait()

    def norm_rows(tok, dst):
        adapted = jnp.dot(tok, aw_ref[...], preferred_element_type=jnp.float32)
        centred = adapted - jnp.mean(adapted, axis=-1, keepdims=True)
        row_var = jnp.mean(centred * centred, axis=-1, keepdims=True)
        normed = centred * lax.rsqrt(row_var + EPSILON) * gain_ref[...].reshape(1, -1)
        hid[dst : dst + PIECE, :] = normed.astype(jnp.bfloat16)

    def head_step(k, i):
        bias = bias_ref[pl.ds(i * TILE, TILE)].reshape(1, TILE)
        logits = jnp.dot(hid[k * HALF : (k + 1) * HALF, :], wbuf[i], preferred_element_type=jnp.float32)
        x = jnp.maximum(jnp.max(logits.reshape(8, LEN, TILE), axis=1) + bias, 0.0)
        for _ in range(3):
            x = x * (x + 2.0)
        for q in range(TILE // BLOCK):
            pooled[k, i * (TILE // BLOCK) + q] = x[:, q * BLOCK : (q + 1) * BLOCK]

    def tiles_of(k, o):
        at = starts[o]
        two = jnp.concatenate(
            [pooled[k, at], pooled[k, jnp.minimum(at + 1, NB - 1)]], axis=0
        )
        send[k, o] = two.astype(jnp.bfloat16)

    def send_tiles(k, half):
        def one(t, carry):
            o = (d + t) % OWNERS
            tiles_of(k, o)
            pltpu.make_async_remote_copy(
                src_ref=send.at[k, o],
                dst_ref=recv_ref.at[half, d],
                send_sem=tile_send.at[k],
                recv_sem=tile_recv.at[k],
                device_id=(o, v),
                device_id_type=MESH,
            ).start()
            return carry

        lax.fori_loop(1, OWNERS, one, 0)
        tiles_of(k, d)
        pltpu.make_async_copy(send.at[k, d], recv_ref.at[half, d], tile_own.at[k]).start()

    for r, partner in enumerate(near):
        token_copy(r, v, partner).wait_recv()
    tok = near_tok[...].reshape(HALF, BLOCK)
    for i in range(STEPS):
        norm_rows(tok[i * PIECE : (i + 1) * PIECE], i * PIECE)
    for r, partner in enumerate(far):
        token_copy(r + 3, v, partner).wait_recv()
    tok = far_tok[...].reshape(HALF, BLOCK)
    for i in range(STEPS):
        weight_copy(i).wait()
        head_step(0, i)
        norm_rows(tok[i * PIECE : (i + 1) * PIECE], HALF + i * PIECE)
    send_tiles(0, pair)

    def head_second(i, carry):
        head_step(1, i)
        return carry

    lax.fori_loop(0, STEPS, head_second, 0)
    send_tiles(1, 1 - pair)

    for r, partner in enumerate(near + far):
        token_copy(r, partner, v).wait_send()
    for k, half in enumerate((pair, 1 - pair)):
        pltpu.make_async_copy(send.at[k, d], recv_ref.at[half, d], tile_own.at[k]).wait()
        others = send.at[k, 0 : OWNERS - 1]
        pltpu.make_async_copy(others, others, tile_send.at[k]).wait()
        others = recv_ref.at[half, 0 : OWNERS - 1]
        pltpu.make_async_copy(others, others, tile_recv.at[k]).wait()


def scale_kernel(counts_ref, code_ref, out_ref):
    owner = lax.axis_index("docs")
    count = counts_ref[0, owner]
    for s in range(2):
        code = code_ref[:, :, s * 8 : (s + 1) * 8, :].astype(jnp.float32)
        top = jnp.max(code.reshape(-1, 8, BLOCK), axis=0)
        top = jnp.max(top, axis=0, keepdims=True)
        peak = jnp.maximum(jnp.log1p(top) * 0.125, 1.0)
        factor = jnp.where(s < count, 0.125 / peak, 0.0)
        for h in range(2):
            out_ref[s, :, h] = jnp.log1p(code[h]) * factor


def shards(tokens, token_mask, adapter_weight, norm_gain, head_weight, head_bias, block_counts):
    vmem = pl.BlockSpec(memory_space=pltpu.VMEM)
    smem = pl.BlockSpec(memory_space=pltpu.SMEM)
    hbm = pl.BlockSpec(memory_space=pltpu.HBM)
    codes = pl.pallas_call(
        index_kernel,
        out_shape=jax.ShapeDtypeStruct((2, OWNERS, 16, BLOCK), jnp.bfloat16),
        in_specs=[hbm] * 7,
        out_specs=pl.BlockSpec(memory_space=pl.ANY),
        scratch_shapes=[
            pltpu.VMEM((2, LEN, BLOCK), jnp.bfloat16),
            pltpu.VMEM((2, LEN), jnp.int32),
            pltpu.VMEM((BLOCK, 768), jnp.bfloat16),
            pltpu.VMEM((768,), jnp.float32),
            pltpu.VMEM((NB * BLOCK,), jnp.float32),
            pltpu.SMEM((1, OWNERS), jnp.int32),
            pltpu.VMEM((4, SHARD, BLOCK), jnp.bfloat16),
            pltpu.VMEM((4, SHARD, BLOCK), jnp.bfloat16),
            pltpu.VMEM((2 * HALF, 768), jnp.bfloat16),
            pltpu.VMEM((STEPS, 768, TILE), jnp.bfloat16),
            pltpu.VMEM((2, NB, 8, BLOCK), jnp.float32),
            pltpu.VMEM((2, OWNERS, 16, BLOCK), jnp.bfloat16),
            pltpu.SMEM((OWNERS,), jnp.int32),
            pltpu.SemaphoreType.DMA((6,)),
            pltpu.SemaphoreType.DMA((STEPS,)),
            pltpu.SemaphoreType.DMA((7,)),
            pltpu.SemaphoreType.DMA((7,)),
            pltpu.SemaphoreType.DMA((2,)),
            pltpu.SemaphoreType.DMA((2,)),
            pltpu.SemaphoreType.DMA((2,)),
        ],
        compiler_params=pltpu.CompilerParams(
            collective_id=0, has_side_effects=True, vmem_limit_bytes=48 * 2**20
        ),
        cost_estimate=pl.CostEstimate(
            flops=8_000_000_000, bytes_accessed=7_000_000, transcendentals=0
        ),
        name="index",
    )(*(
        pltpu.with_memory_space_constraint(x, pltpu.HBM)
        for x in (
            tokens, token_mask, adapter_weight, norm_gain, head_bias, block_counts, head_weight
        )
    ))
    scaled = pl.pallas_call(
        scale_kernel,
        out_shape=jax.ShapeDtypeStruct((2, OWNERS, 2, 8, BLOCK), jnp.float32),
        in_specs=[smem, vmem],
        out_specs=vmem,
        compiler_params=pltpu.CompilerParams(vmem_limit_bytes=8 * 2**20),
        cost_estimate=pl.CostEstimate(flops=4_000_000, bytes_accessed=800_000, transcendentals=131072),
        name="scale",
    )(block_counts, codes)
    return scaled.reshape(2, OWNERS * 16, BLOCK)


def solution(mesh):
    in_specs = (
        P(("docs", "vocab"), None, None),
        P(("docs", "vocab"), None),
        P(),
        P(),
        P(None, "vocab"),
        P("vocab"),
        P("vocab", None),
    )
    out_specs = P("docs", None, "vocab")
    return jax.shard_map(shards, mesh=mesh, in_specs=in_specs, out_specs=out_specs, check_vma=False)
```

```python
import functools

import jax
import jax.numpy as jnp
from jax import lax
from jax.experimental import pallas as pl
from jax.experimental.pallas import tpu as pltpu
from jax.sharding import PartitionSpec as P

MESH = pl.DeviceIdType.MESH
BLOCK = 128
EPSILON = 1e-05
OWNERS = 32
CHIPS_Y = 4
NB = 30
LEN = 80
SHARD = 2 * LEN
CHUNK = 2 * SHARD
TILE = 768
STEPS = NB * BLOCK // TILE
PIECE = CHUNK // STEPS


def index_kernel(
    tok_hbm, mask_hbm, aw_hbm, gain_hbm, bias_hbm, counts_hbm, hw_hbm, recv_ref,
    tok_ref, mask_ref, aw_ref, gain_ref, bias_ref, counts_ref,
    tok_a, tok_b, tok_c, tok_d, hid, wbuf, pooled, send, starts,
    arg_sem, wsem, tok_send, tok_recv, ready, tile_send, tile_recv, tile_own,
):
    d = lax.axis_index("docs")
    v = lax.axis_index("vocab")
    y = v // 2
    c = v % 2
    y1 = y + 1 - 2 * (y % 2)
    y3 = CHIPS_Y - 1 - y
    sibling, near, far = y * 2 + 1 - c, y1 * 2 + c, y3 * 2 + c
    flips = [d + 2**b - 2 ** (b + 1) * ((d // 2**b) % 2) for b in range(5)]

    arg_copies = [
        pltpu.make_async_copy(src, dst, arg_sem.at[i])
        for i, (src, dst) in enumerate((
            (tok_hbm, tok_ref), (mask_hbm, mask_ref), (aw_hbm, aw_ref),
            (gain_hbm, gain_ref), (bias_hbm, bias_ref), (counts_hbm, counts_ref),
        ))
    ]
    for copy in arg_copies:
        copy.start()

    def weight_copy(i):
        cols = slice(i * TILE, (i + 1) * TILE)
        return pltpu.make_async_copy(hw_hbm.at[:, cols], wbuf.at[i], wsem.at[i])

    barrier = pltpu.get_barrier_semaphore()
    for partner in (sibling, near, far):
        pl.semaphore_signal(barrier, inc=1, device_id=(d, partner), device_id_type=MESH)
    for partner in flips:
        pl.semaphore_signal(barrier, inc=1, device_id=(partner, v), device_id_type=MESH)
    for i in range(STEPS):
        weight_copy(i).start()

    slot = lax.broadcasted_iota(jnp.int32, (LEN, BLOCK), 0).astype(jnp.float32)
    arg_copies[0].wait()
    arg_copies[1].wait()
    for p in range(2):
        live = jnp.sum(mask_ref[p : p + 1, :].astype(jnp.float32), axis=1, keepdims=True)
        tok = tok_ref[p].astype(jnp.float32)
        tok = jnp.where(slot < live, tok, tok[0:1, :])
        tok_a[c, p * LEN : (p + 1) * LEN, :] = tok.astype(jnp.bfloat16)

    pl.semaphore_wait(barrier, 8)

    def token_copy(r, src, dst, partner, core):
        return pltpu.make_async_remote_copy(
            src_ref=src.at[core],
            dst_ref=dst.at[core],
            send_sem=tok_send.at[r],
            recv_sem=tok_recv.at[r],
            device_id=(d, partner),
            device_id_type=MESH,
        )

    own_sibling = token_copy(0, tok_a, tok_a, sibling, c)
    own_near = token_copy(1, tok_a, tok_b, near, c)
    own_far = token_copy(2, tok_a, tok_c, far, c)
    near_sibling = token_copy(3, tok_b, tok_b, sibling, c)
    near_far = token_copy(4, tok_b, tok_d, far, c)
    far_sibling = token_copy(5, tok_c, tok_c, sibling, c)
    across_sibling = token_copy(6, tok_d, tok_d, sibling, c)
    own_sibling.start()
    own_near.start()
    own_far.start()

    def from_sibling(r, buf):
        token_copy(r, buf, buf, sibling, 1 - c).wait_recv()

    def tell(b):
        pl.semaphore_signal(ready.at[b - 1], inc=1, device_id=(flips[b], v), device_id_type=MESH)

    tell(1)
    arg_copies[5].wait()

    def note_start(o, at):
        starts[o] = jnp.minimum(at, NB - 1)
        return at + counts_ref[0, o]

    lax.fori_loop(0, OWNERS, note_start, jnp.int32(0))
    for i in (2, 3, 4):
        arg_copies[i].wait()

    def norm_rows(tok, chunk, at):
        adapted = jnp.dot(tok, aw_ref[...], preferred_element_type=jnp.float32)
        centred = adapted - jnp.mean(adapted, axis=-1, keepdims=True)
        row_var = jnp.mean(centred * centred, axis=-1, keepdims=True)
        normed = centred * lax.rsqrt(row_var + EPSILON) * gain_ref[...].reshape(1, -1)
        hid[chunk, at : at + tok.shape[0], :] = normed.astype(jnp.bfloat16)

    def head_step(chunk, i):
        bias = bias_ref[i * TILE : (i + 1) * TILE].reshape(1, TILE)
        logits = jnp.dot(hid[chunk], wbuf[i], preferred_element_type=jnp.float32)
        x = jnp.maximum(jnp.max(logits.reshape(4, LEN, TILE), axis=1) + bias, 0.0)
        for _ in range(3):
            x = x * (x + 2.0)
        row = chunk % 2 * 4
        for q in range(TILE // BLOCK):
            pooled[chunk // 2, i * (TILE // BLOCK) + q, row : row + 4] = x[:, q * BLOCK : (q + 1) * BLOCK]

    def tiles_of(k, o):
        at = starts[o]
        two = jnp.concatenate(
            [pooled[k, at], pooled[k, jnp.minimum(at + 1, NB - 1)]], axis=0
        )
        send[k, o] = two.astype(jnp.bfloat16)

    def send_tile(k, t):
        o = (d + t) % OWNERS
        tiles_of(k, o)
        pltpu.make_async_remote_copy(
            src_ref=send.at[k, o],
            dst_ref=recv_ref.at[k, d],
            send_sem=tile_send.at[k],
            recv_sem=tile_recv.at[k],
            device_id=(o, v),
            device_id_type=MESH,
        ).start()

    def keep_tile(k):
        tiles_of(k, d)
        pltpu.make_async_copy(send.at[k, d], recv_ref.at[k, d], tile_own.at[k]).start()

    from_sibling(0, tok_a)
    tok = tok_a[...].reshape(CHUNK, BLOCK)
    for i in range(STEPS):
        norm_rows(tok[i * PIECE : (i + 1) * PIECE], 0, i * PIECE)
    own_near.wait_recv()
    near_sibling.start()
    near_far.start()
    pl.semaphore_wait(ready.at[0], 1)
    tell(2)

    for i in range(STEPS):
        weight_copy(i).wait()
        if i == 1:
            from_sibling(3, tok_b)
            tok = tok_b[...].reshape(CHUNK, BLOCK)
        head_step(0, i)
        if i >= 1:
            rows = CHUNK // (STEPS - 1)
            norm_rows(tok[(i - 1) * rows : i * rows], 1, (i - 1) * rows)
    pl.semaphore_wait(ready.at[1], 1)
    tell(3)
    own_far.wait_recv()
    far_sibling.start()
    token_copy(4, tok_b, tok_d, far, c).wait_recv()
    across_sibling.start()

    for i in range(STEPS):
        if i == 1:
            pl.semaphore_wait(ready.at[2], 1)
            tell(4)
            from_sibling(5, tok_c)
            tok = tok_c[...].reshape(CHUNK, BLOCK)
        head_step(1, i)
        if i >= 1:
            norm_rows(tok[(i - 1) * rows : i * rows], 2, (i - 1) * rows)
    pl.semaphore_wait(ready.at[3], 1)
    from_sibling(6, tok_d)
    tok = tok_d[...].reshape(CHUNK, BLOCK)

    for i in range(STEPS):
        head_step(2, i)
        norm_rows(tok[i * PIECE : (i + 1) * PIECE], 3, i * PIECE)
        for t in range(1 + i, OWNERS, STEPS):
            send_tile(0, t)
    keep_tile(0)
    for i in range(STEPS):
        head_step(3, i)

    def send_second(t, carry):
        send_tile(1, t)
        return carry

    lax.fori_loop(1, OWNERS, send_second, 0)
    keep_tile(1)

    for copy in (own_sibling, own_near, own_far, near_sibling, near_far, far_sibling, across_sibling):
        copy.wait_send()
    for k in range(2):
        pltpu.make_async_copy(send.at[k, d], recv_ref.at[k, d], tile_own.at[k]).wait()
        others = send.at[k, 0 : OWNERS - 1]
        pltpu.make_async_copy(others, others, tile_send.at[k]).wait()
        others = recv_ref.at[k, 0 : OWNERS - 1]
        pltpu.make_async_copy(others, others, tile_recv.at[k]).wait()


def scale_kernel(counts_ref, code_ref, out_ref):
    owner = lax.axis_index("docs")
    y = lax.axis_index("vocab") // 2
    count = counts_ref[0, owner]
    for s in range(2):
        code = code_ref[:, :, s * 8 : (s + 1) * 8, :].astype(jnp.float32)
        top = jnp.max(code.reshape(-1, 8, BLOCK), axis=0)
        top = jnp.max(top, axis=0, keepdims=True)
        peak = jnp.maximum(jnp.log1p(top) * 0.125, 1.0)
        factor = jnp.where(s < count, 0.125 / peak, 0.0)
        for h in range(2):
            rows = jnp.log1p(code[h]) * factor
            swapped = jnp.concatenate([rows[:, 4:], rows[:, :4]], axis=1)
            half = y // 2 if h == 0 else 1 - y // 2
            out_ref[s, :, half] = jnp.where(y % 2 == 1 - h, swapped, rows)


def shards(tokens, token_mask, adapter_weight, norm_gain, head_weight, head_bias, block_counts):
    vmem = pl.BlockSpec(memory_space=pltpu.VMEM)
    smem = pl.BlockSpec(memory_space=pltpu.SMEM)
    hbm = pl.BlockSpec(memory_space=pltpu.HBM)
    codes = pl.pallas_call(
        index_kernel,
        out_shape=jax.ShapeDtypeStruct((2, OWNERS, 16, BLOCK), jnp.bfloat16),
        in_specs=[hbm] * 7,
        out_specs=pl.BlockSpec(memory_space=pl.ANY),
        scratch_shapes=[
            pltpu.VMEM((2, LEN, BLOCK), jnp.bfloat16),
            pltpu.VMEM((2, LEN), jnp.int32),
            pltpu.VMEM((BLOCK, 768), jnp.bfloat16),
            pltpu.VMEM((768,), jnp.float32),
            pltpu.VMEM((NB * BLOCK,), jnp.float32),
            pltpu.SMEM((1, OWNERS), jnp.int32),
            pltpu.VMEM((2, SHARD, BLOCK), jnp.bfloat16),
            pltpu.VMEM((2, SHARD, BLOCK), jnp.bfloat16),
            pltpu.VMEM((2, SHARD, BLOCK), jnp.bfloat16),
            pltpu.VMEM((2, SHARD, BLOCK), jnp.bfloat16),
            pltpu.VMEM((4, CHUNK, 768), jnp.bfloat16),
            pltpu.VMEM((STEPS, 768, TILE), jnp.bfloat16),
            pltpu.VMEM((2, NB, 8, BLOCK), jnp.float32),
            pltpu.VMEM((2, OWNERS, 16, BLOCK), jnp.bfloat16),
            pltpu.SMEM((OWNERS,), jnp.int32),
            pltpu.SemaphoreType.DMA((6,)),
            pltpu.SemaphoreType.DMA((STEPS,)),
            pltpu.SemaphoreType.DMA((7,)),
            pltpu.SemaphoreType.DMA((7,)),
            pltpu.SemaphoreType.REGULAR((4,)),
            pltpu.SemaphoreType.DMA((2,)),
            pltpu.SemaphoreType.DMA((2,)),
            pltpu.SemaphoreType.DMA((2,)),
        ],
        compiler_params=pltpu.CompilerParams(
            collective_id=0, has_side_effects=True, vmem_limit_bytes=48 * 2**20
        ),
        cost_estimate=pl.CostEstimate(
            flops=8_000_000_000, bytes_accessed=7_000_000, transcendentals=0
        ),
        name="index",
    )(*(
        pltpu.with_memory_space_constraint(x, pltpu.HBM)
        for x in (
            tokens, token_mask, adapter_weight, norm_gain, head_bias, block_counts, head_weight
        )
    ))
    scaled = pl.pallas_call(
        scale_kernel,
        out_shape=jax.ShapeDtypeStruct((2, OWNERS, 2, 8, BLOCK), jnp.float32),
        in_specs=[smem, vmem],
        out_specs=vmem,
        compiler_params=pltpu.CompilerParams(vmem_limit_bytes=8 * 2**20),
        cost_estimate=pl.CostEstimate(flops=4_000_000, bytes_accessed=800_000, transcendentals=131072),
        name="scale",
    )(block_counts, codes)
    return scaled.reshape(2, OWNERS * 16, BLOCK)


def solution(mesh):
    in_specs = (
        P(("docs", "vocab"), None, None),
        P(("docs", "vocab"), None),
        P(),
        P(),
        P(None, "vocab"),
        P("vocab"),
        P("vocab", None),
    )
    out_specs = P("docs", None, "vocab")
    return jax.shard_map(shards, mesh=mesh, in_specs=in_specs, out_specs=out_specs, check_vma=False)
```

```python
import functools

import jax
import jax.numpy as jnp
from jax import lax
from jax.experimental import pallas as pl
from jax.experimental.pallas import tpu as pltpu
from jax.sharding import PartitionSpec as P

MESH = pl.DeviceIdType.MESH
BLOCK = 128
EPSILON = 1e-05
OWNERS = 32
CHIPS_Y = 4
SIZE_X = 4
SIZE_Z = 8
NB = 30
LEN = 80
SHARD = 2 * LEN
CHUNK = 2 * SHARD
TILE = 768
STEPS = NB * BLOCK // TILE


def index_kernel(
    tok_hbm, mask_hbm, aw_hbm, gain_hbm, bias_hbm, counts_hbm, hw_hbm, recv_ref,
    tok_ref, mask_ref, aw_ref, gain_ref, bias_ref, counts_ref,
    tok_a, tok_b, tok_c, tok_d, hid, wbuf, pooled, send, starts,
    arg_sem, wsem, tok_send, tok_recv, ready, tile_send, tile_recv, tile_own,
):
    d = lax.axis_index("docs")
    v = lax.axis_index("vocab")
    y = v // 2
    c = v % 2
    y1 = y + 1 - 2 * (y % 2)
    y2 = (y + 2) % CHIPS_Y
    y3 = CHIPS_Y - 1 - y
    partners = [y * 2 + 1 - c] + [chip * 2 + core for chip in (y1, y3, y2) for core in (c, 1 - c)]
    x = d // SIZE_Z
    z = d % SIZE_Z

    def across(dx, dz):
        return (x + dx) % SIZE_X * SIZE_Z + (z + dz) % SIZE_Z


    arg_copies = [
        pltpu.make_async_copy(src, dst, arg_sem.at[i])
        for i, (src, dst) in enumerate((
            (tok_hbm, tok_ref), (mask_hbm, mask_ref), (aw_hbm, aw_ref),
            (gain_hbm, gain_ref), (bias_hbm, bias_ref), (counts_hbm, counts_ref),
        ))
    ]
    for copy in arg_copies:
        copy.start()

    def weight_copy(i):
        cols = slice(i * TILE, (i + 1) * TILE)
        return pltpu.make_async_copy(hw_hbm.at[:, cols], wbuf.at[i], wsem.at[i])

    barrier = pltpu.get_barrier_semaphore()
    for partner in partners:
        pl.semaphore_signal(barrier, inc=1, device_id=(d, partner), device_id_type=MESH)
    for dx, dz in ((0, 1), (0, -1), (1, 0), (-1, 0)):
        pl.semaphore_signal(barrier, inc=1, device_id=(across(dx, dz), v), device_id_type=MESH)
    for i in range(STEPS):
        weight_copy(i).start()

    slot = lax.broadcasted_iota(jnp.int32, (LEN, BLOCK), 0).astype(jnp.float32)
    arg_copies[0].wait()
    arg_copies[1].wait()
    for p in range(2):
        live = jnp.sum(mask_ref[p : p + 1, :].astype(jnp.float32), axis=1, keepdims=True)
        tok = tok_ref[p].astype(jnp.float32)
        tok = jnp.where(slot < live, tok, tok[0:1, :])
        tok_a[c, p * LEN : (p + 1) * LEN, :] = tok.astype(jnp.bfloat16)

    pl.semaphore_wait(barrier, 11)

    buffers = [tok_a, tok_b, tok_b, tok_c, tok_c, tok_d, tok_d]

    def token_copy(r, core):
        return pltpu.make_async_remote_copy(
            src_ref=tok_a.at[core],
            dst_ref=buffers[r].at[core],
            send_sem=tok_send.at[r],
            recv_sem=tok_recv.at[r],
            device_id=(d, partners[r]),
            device_id_type=MESH,
        )

    def tokens_in(r):
        token_copy(r, c if r in (1, 3, 5) else 1 - c).wait_recv()

    def tell(r):
        for way, step in enumerate((1, -1)[: 1 if r == 4 else 2]):
            to = across(0, step) if r < 3 else across(step, 0)
            pl.semaphore_signal(ready.at[r, way], inc=1, device_id=(to, v), device_id_type=MESH)

    def told(r):
        for way in range(1 if r == 4 else 2):
            pl.semaphore_wait(ready.at[r, way], 1)

    for r in range(5):
        token_copy(r, c).start()
    tell(0)
    arg_copies[5].wait()

    def note_start(o, at):
        starts[o] = jnp.minimum(at, NB - 1)
        return at + counts_ref[0, o]

    lax.fori_loop(0, OWNERS, note_start, jnp.int32(0))
    for i in (2, 3, 4):
        arg_copies[i].wait()

    def norm_rows(tok, chunk, at):
        adapted = jnp.dot(tok, aw_ref[...], preferred_element_type=jnp.float32)
        centred = adapted - jnp.mean(adapted, axis=-1, keepdims=True)
        row_var = jnp.mean(centred * centred, axis=-1, keepdims=True)
        normed = centred * lax.rsqrt(row_var + EPSILON) * gain_ref[...].reshape(1, -1)
        hid[chunk, at : at + tok.shape[0], :] = normed.astype(jnp.bfloat16)

    def head_step(chunk, i):
        bias = bias_ref[i * TILE : (i + 1) * TILE].reshape(1, TILE)
        logits = jnp.dot(hid[chunk], wbuf[i], preferred_element_type=jnp.float32)
        x = jnp.maximum(jnp.max(logits.reshape(4, LEN, TILE), axis=1) + bias, 0.0)
        for _ in range(3):
            x = x * (x + 2.0)
        row = chunk % 2 * 4
        for q in range(TILE // BLOCK):
            pooled[chunk // 2, i * (TILE // BLOCK) + q, row : row + 4] = x[:, q * BLOCK : (q + 1) * BLOCK]

    def tiles_of(k, o):
        at = starts[o]
        two = jnp.concatenate(
            [pooled[k, at], pooled[k, jnp.minimum(at + 1, NB - 1)]], axis=0
        )
        send[k, o] = two.astype(jnp.bfloat16)

    def hops(t):
        dx, dz = t
        return min(dx, SIZE_X - dx) + min(dz, SIZE_Z - dz)

    owners = sorted(
        ((dx, dz) for dx in range(SIZE_X) for dz in range(SIZE_Z) if dx or dz), key=hops, reverse=True
    )

    def send_tile(k, t):
        o = across(*t)
        tiles_of(k, o)
        pltpu.make_async_remote_copy(
            src_ref=send.at[k, o],
            dst_ref=recv_ref.at[k, d],
            send_sem=tile_send.at[k],
            recv_sem=tile_recv.at[k],
            device_id=(o, v),
            device_id_type=MESH,
        ).start()

    def keep_tile(k):
        tiles_of(k, d)
        pltpu.make_async_copy(send.at[k, d], recv_ref.at[k, d], tile_own.at[k]).start()

    def norm_chunk(chunk, buf, piece, pieces):
        rows = CHUNK // pieces
        tok = buf[piece * rows // SHARD, piece * rows % SHARD : piece * rows % SHARD + rows, :]
        norm_rows(tok, chunk, piece * rows)

    tokens_in(0)
    for i in range(4):
        norm_chunk(0, tok_a, i, 4)
    for r in (5, 6):
        token_copy(r, c).start()
    told(0)
    tell(1)
    for i in range(STEPS):
        weight_copy(i).wait()
        head_step(0, i)
        if i == 2:
            told(1)
            tell(2)

    told(2)
    tell(3)
    tokens_in(1)
    tokens_in(2)
    for i in range(4):
        norm_chunk(1, tok_b, i, 4)
    tokens_in(3)
    tokens_in(4)
    for i in range(STEPS):
        head_step(1, i)
        if i < 4:
            norm_chunk(2, tok_c, i, 4)
        if i == 1:
            told(3)
            tell(4)
    told(4)
    tokens_in(5)
    tokens_in(6)

    for i in range(STEPS):
        head_step(2, i)
        if i < 4:
            norm_chunk(3, tok_d, i, 4)
        for t in owners[i * 7 : i * 7 + 7]:
            send_tile(0, t)
    keep_tile(0)
    for i in range(STEPS):
        head_step(3, i)
    for t in owners:
        send_tile(1, t)
    keep_tile(1)

    for r in range(7):
        token_copy(r, c).wait_send()
    for k in range(2):
        pltpu.make_async_copy(send.at[k, d], recv_ref.at[k, d], tile_own.at[k]).wait()
        others = send.at[k, 0 : OWNERS - 1]
        pltpu.make_async_copy(others, others, tile_send.at[k]).wait()
        others = recv_ref.at[k, 0 : OWNERS - 1]
        pltpu.make_async_copy(others, others, tile_recv.at[k]).wait()


def scale_kernel(counts_ref, code_ref, out_ref):
    owner = lax.axis_index("docs")
    y = lax.axis_index("vocab") // 2
    count = counts_ref[0, owner]
    for s in range(2):
        code = code_ref[:, :, s * 8 : (s + 1) * 8, :].astype(jnp.float32)
        top = jnp.max(code.reshape(-1, 8, BLOCK), axis=0)
        top = jnp.max(top, axis=0, keepdims=True)
        peak = jnp.maximum(jnp.log1p(top) * 0.125, 1.0)
        factor = jnp.where(s < count, 0.125 / peak, 0.0)
        for h in range(2):
            rows = jnp.log1p(code[h]) * factor
            swapped = jnp.concatenate([rows[:, 4:], rows[:, :4]], axis=1)
            half = y // 2 if h == 0 else 1 - y // 2
            out_ref[s, :, half] = jnp.where(y % 2 == 1 - h, swapped, rows)


def shards(tokens, token_mask, adapter_weight, norm_gain, head_weight, head_bias, block_counts):
    vmem = pl.BlockSpec(memory_space=pltpu.VMEM)
    smem = pl.BlockSpec(memory_space=pltpu.SMEM)
    hbm = pl.BlockSpec(memory_space=pltpu.HBM)
    codes = pl.pallas_call(
        index_kernel,
        out_shape=jax.ShapeDtypeStruct((2, OWNERS, 16, BLOCK), jnp.bfloat16),
        in_specs=[hbm] * 7,
        out_specs=pl.BlockSpec(memory_space=pl.ANY),
        scratch_shapes=[
            pltpu.VMEM((2, LEN, BLOCK), jnp.bfloat16),
            pltpu.VMEM((2, LEN), jnp.int32),
            pltpu.VMEM((BLOCK, 768), jnp.bfloat16),
            pltpu.VMEM((768,), jnp.float32),
            pltpu.VMEM((NB * BLOCK,), jnp.float32),
            pltpu.SMEM((1, OWNERS), jnp.int32),
            pltpu.VMEM((2, SHARD, BLOCK), jnp.bfloat16),
            pltpu.VMEM((2, SHARD, BLOCK), jnp.bfloat16),
            pltpu.VMEM((2, SHARD, BLOCK), jnp.bfloat16),
            pltpu.VMEM((2, SHARD, BLOCK), jnp.bfloat16),
            pltpu.VMEM((4, CHUNK, 768), jnp.bfloat16),
            pltpu.VMEM((STEPS, 768, TILE), jnp.bfloat16),
            pltpu.VMEM((2, NB, 8, BLOCK), jnp.float32),
            pltpu.VMEM((2, OWNERS, 16, BLOCK), jnp.bfloat16),
            pltpu.SMEM((OWNERS,), jnp.int32),
            pltpu.SemaphoreType.DMA((6,)),
            pltpu.SemaphoreType.DMA((STEPS,)),
            pltpu.SemaphoreType.DMA((7,)),
            pltpu.SemaphoreType.DMA((7,)),
            pltpu.SemaphoreType.REGULAR((5, 2)),
            pltpu.SemaphoreType.DMA((2,)),
            pltpu.SemaphoreType.DMA((2,)),
            pltpu.SemaphoreType.DMA((2,)),
        ],
        compiler_params=pltpu.CompilerParams(
            collective_id=0, has_side_effects=True, vmem_limit_bytes=48 * 2**20
        ),
        cost_estimate=pl.CostEstimate(
            flops=8_000_000_000, bytes_accessed=7_000_000, transcendentals=0
        ),
        name="index",
    )(*(
        pltpu.with_memory_space_constraint(x, pltpu.HBM)
        for x in (
            tokens, token_mask, adapter_weight, norm_gain, head_bias, block_counts, head_weight
        )
    ))
    scaled = pl.pallas_call(
        scale_kernel,
        out_shape=jax.ShapeDtypeStruct((2, OWNERS, 2, 8, BLOCK), jnp.float32),
        in_specs=[smem, vmem],
        out_specs=vmem,
        compiler_params=pltpu.CompilerParams(vmem_limit_bytes=8 * 2**20),
        cost_estimate=pl.CostEstimate(flops=4_000_000, bytes_accessed=800_000, transcendentals=131072),
        name="scale",
    )(block_counts, codes)
    return scaled.reshape(2, OWNERS * 16, BLOCK)


def solution(mesh):
    in_specs = (
        P(("docs", "vocab"), None, None),
        P(("docs", "vocab"), None),
        P(),
        P(),
        P(None, "vocab"),
        P("vocab"),
        P("vocab", None),
    )
    out_specs = P("docs", None, "vocab")
    return jax.shard_map(shards, mesh=mesh, in_specs=in_specs, out_specs=out_specs, check_vma=False)
```

```python
import functools

import jax
import jax.numpy as jnp
from jax import lax
from jax.experimental import pallas as pl
from jax.experimental.pallas import tpu as pltpu
from jax.sharding import PartitionSpec as P

MESH = pl.DeviceIdType.MESH
BLOCK = 128
EPSILON = 1e-05
OWNERS = 32
CHIPS_Y = 4
SIZE_X = 4
SIZE_Z = 8
NB = 30
LEN = 80
SHARD = 2 * LEN
CHUNK = 2 * SHARD
TILE = 768
STEPS = NB * BLOCK // TILE


def index_kernel(
    tok_hbm, mask_hbm, aw_hbm, gain_hbm, bias_hbm, counts_hbm, hw_hbm, recv_ref,
    tok_ref, mask_ref, aw_ref, gain_ref, bias_ref, counts_ref,
    tok_own, tok_a, tok_b, tok_c, tok_d, hid, wbuf, pooled, send, starts,
    arg_sem, wsem, tok_send, tok_recv, ready, tile_send, tile_recv, tile_own,
):
    d = lax.axis_index("docs")
    v = lax.axis_index("vocab")
    y = v // 2
    c = v % 2
    y1 = y + 1 - 2 * (y % 2)
    y2 = (y + 2) % CHIPS_Y
    y3 = CHIPS_Y - 1 - y
    partners = [y * 2 + 1 - c] + [chip * 2 + core for chip in (y1, y3, y2) for core in (c, 1 - c)]
    x = d // SIZE_Z
    z = d % SIZE_Z

    def across(dx, dz):
        return (x + dx) % SIZE_X * SIZE_Z + (z + dz) % SIZE_Z


    arg_copies = [
        pltpu.make_async_copy(src, dst, arg_sem.at[i])
        for i, (src, dst) in enumerate((
            (tok_hbm, tok_ref), (mask_hbm, mask_ref), (aw_hbm, aw_ref),
            (gain_hbm, gain_ref), (bias_hbm, bias_ref), (counts_hbm, counts_ref),
        ))
    ]
    for copy in arg_copies:
        copy.start()

    def weight_copy(i):
        cols = slice(i * TILE, (i + 1) * TILE)
        return pltpu.make_async_copy(hw_hbm.at[:, cols], wbuf.at[i], wsem.at[i])

    barrier = pltpu.get_barrier_semaphore()
    for partner in partners:
        pl.semaphore_signal(barrier, inc=1, device_id=(d, partner), device_id_type=MESH)
    for dx, dz in ((0, 1), (0, -1), (1, 0), (-1, 0)):
        pl.semaphore_signal(barrier, inc=1, device_id=(across(dx, dz), v), device_id_type=MESH)
    for i in range(STEPS):
        weight_copy(i).start()

    slot = lax.broadcasted_iota(jnp.int32, (LEN, BLOCK), 0).astype(jnp.float32)
    arg_copies[0].wait()
    arg_copies[1].wait()
    for p in range(2):
        live = jnp.sum(mask_ref[p : p + 1, :].astype(jnp.float32), axis=1, keepdims=True)
        tok = tok_ref[p].astype(jnp.float32)
        tok = jnp.where(slot < live, tok, tok[0:1, :])
        tok_own[p * LEN : (p + 1) * LEN, :] = tok.astype(jnp.bfloat16)

    pl.semaphore_wait(barrier, 11)

    buffers = [None, tok_b, tok_b, tok_c, tok_c, tok_d, tok_d]

    def token_copy(r, core):
        return pltpu.make_async_remote_copy(
            src_ref=tok_own,
            dst_ref=tok_a if r == 0 else buffers[r].at[core],
            send_sem=tok_send.at[r],
            recv_sem=tok_recv.at[r],
            device_id=(d, partners[r]),
            device_id_type=MESH,
        )

    def tokens_in(r):
        token_copy(r, c if r in (1, 3, 5) else 1 - c).wait_recv()

    def tell(r):
        for way, step in enumerate((1, -1)[: 1 if r == 4 else 2]):
            to = across(0, step) if r < 3 else across(step, 0)
            pl.semaphore_signal(ready.at[r, way], inc=1, device_id=(to, v), device_id_type=MESH)

    def told(r):
        for way in range(1 if r == 4 else 2):
            pl.semaphore_wait(ready.at[r, way], 1)

    for r in range(5):
        token_copy(r, c).start()
    tell(0)
    arg_copies[5].wait()

    def note_start(o, at):
        starts[o] = jnp.minimum(at, NB - 1)
        return at + counts_ref[0, o]

    lax.fori_loop(0, OWNERS, note_start, jnp.int32(0))
    for i in (2, 3, 4):
        arg_copies[i].wait()

    def norm_rows(tok, chunk, at):
        adapted = jnp.dot(tok, aw_ref[...], preferred_element_type=jnp.float32)
        centred = adapted - jnp.mean(adapted, axis=-1, keepdims=True)
        row_var = jnp.mean(centred * centred, axis=-1, keepdims=True)
        normed = centred * lax.rsqrt(row_var + EPSILON) * gain_ref[...].reshape(1, -1)
        hid[chunk, pl.ds(at, tok.shape[0]), :] = normed.astype(jnp.bfloat16)

    def head_step(chunk, i):
        bias = bias_ref[i * TILE : (i + 1) * TILE].reshape(1, TILE)
        logits = jnp.dot(hid[chunk], wbuf[i], preferred_element_type=jnp.float32)
        x = jnp.maximum(jnp.max(logits.reshape(4, LEN, TILE), axis=1) + bias, 0.0)
        for _ in range(3):
            x = x * (x + 2.0)
        row = chunk % 2 * 4
        for q in range(TILE // BLOCK):
            pooled[chunk // 2, i * (TILE // BLOCK) + q, row : row + 4] = x[:, q * BLOCK : (q + 1) * BLOCK]

    def tiles_of(k, o):
        at = starts[o]
        two = jnp.concatenate(
            [pooled[k, at], pooled[k, jnp.minimum(at + 1, NB - 1)]], axis=0
        )
        send[k, o] = two.astype(jnp.bfloat16)

    def hops(t):
        dx, dz = t
        return min(dx, SIZE_X - dx) + min(dz, SIZE_Z - dz)

    owners = sorted(
        ((dx, dz) for dx in range(SIZE_X) for dz in range(SIZE_Z) if dx or dz), key=hops, reverse=True
    )

    def send_tile(k, t):
        o = across(*t)
        tiles_of(k, o)
        pltpu.make_async_remote_copy(
            src_ref=send.at[k, o],
            dst_ref=recv_ref.at[k, d],
            send_sem=tile_send.at[k],
            recv_sem=tile_recv.at[k],
            device_id=(o, v),
            device_id_type=MESH,
        ).start()

    def keep_tile(k):
        tiles_of(k, d)
        pltpu.make_async_copy(send.at[k, d], recv_ref.at[k, d], tile_own.at[k]).start()

    def norm_chunk(chunk, buf, piece, pieces):
        rows = CHUNK // pieces
        tok = buf[piece * rows // SHARD, piece * rows % SHARD : piece * rows % SHARD + rows, :]
        norm_rows(tok, chunk, piece * rows)

    for i in range(2):
        norm_rows(tok_own[i * LEN : (i + 1) * LEN], 0, pl.multiple_of(c * SHARD + i * LEN, 16))
    tokens_in(0)
    for r in (5, 6):
        token_copy(r, c).start()
    for i in range(2):
        norm_rows(tok_a[i * LEN : (i + 1) * LEN], 0, pl.multiple_of((1 - c) * SHARD + i * LEN, 16))
    told(0)
    tell(1)
    for i in range(STEPS):
        weight_copy(i).wait()
    for i in range(STEPS):
        head_step(0, i)

    tokens_in(1)
    tokens_in(2)
    told(1)
    tell(2)
    for i in range(4):
        norm_chunk(1, tok_b, i, 4)
    tokens_in(3)
    tokens_in(4)
    told(2)
    tell(3)
    for i in range(STEPS):
        head_step(1, i)
        if i < 4:
            norm_chunk(2, tok_c, i, 4)
    tokens_in(5)
    tokens_in(6)
    told(3)
    tell(4)
    for i in range(STEPS):
        head_step(2, i)
        if i < 4:
            norm_chunk(3, tok_d, i, 4)
    told(4)

    for t in owners:
        send_tile(0, t)
    for i in range(STEPS):
        head_step(3, i)
    keep_tile(0)
    for t in owners:
        send_tile(1, t)
    keep_tile(1)

    for r in range(7):
        token_copy(r, c).wait_send()
    for k in range(2):
        pltpu.make_async_copy(send.at[k, d], recv_ref.at[k, d], tile_own.at[k]).wait()
        others = send.at[k, 0 : OWNERS - 1]
        pltpu.make_async_copy(others, others, tile_send.at[k]).wait()
        others = recv_ref.at[k, 0 : OWNERS - 1]
        pltpu.make_async_copy(others, others, tile_recv.at[k]).wait()


def scale_kernel(counts_ref, code_ref, out_hbm, out, sem):
    owner = lax.axis_index("docs")
    y = lax.axis_index("vocab") // 2
    count = counts_ref[0, owner]
    copies = []
    for s in range(2):
        code = code_ref[:, :, s * 8 : (s + 1) * 8, :].astype(jnp.float32)
        top = jnp.max(code.reshape(-1, 8, BLOCK), axis=0)
        top = jnp.max(top, axis=0, keepdims=True)
        peak = jnp.maximum(jnp.log1p(top) * 0.125, 1.0)
        factor = jnp.where(s < count, 0.125 / peak, 0.0)
        for h in range(2):
            rows = jnp.log1p(code[h]) * factor
            swapped = jnp.concatenate([rows[:, 4:], rows[:, :4]], axis=1)
            out[s, h] = jnp.where(y % 2 == 1 - h, swapped, rows)
            half = y // 2 if h == 0 else 1 - y // 2
            copy = pltpu.make_async_copy(out.at[s, h], out_hbm.at[s, :, half], sem.at[s, h])
            copy.start()
            copies.append(copy)
    for copy in copies:
        copy.wait()


def shards(tokens, token_mask, adapter_weight, norm_gain, head_weight, head_bias, block_counts):
    vmem = pl.BlockSpec(memory_space=pltpu.VMEM)
    smem = pl.BlockSpec(memory_space=pltpu.SMEM)
    hbm = pl.BlockSpec(memory_space=pltpu.HBM)
    codes = pl.pallas_call(
        index_kernel,
        out_shape=jax.ShapeDtypeStruct((2, OWNERS, 16, BLOCK), jnp.bfloat16),
        in_specs=[hbm] * 7,
        out_specs=pl.BlockSpec(memory_space=pl.ANY),
        scratch_shapes=[
            pltpu.VMEM((2, LEN, BLOCK), jnp.bfloat16),
            pltpu.VMEM((2, LEN), jnp.int32),
            pltpu.VMEM((BLOCK, 768), jnp.bfloat16),
            pltpu.VMEM((768,), jnp.float32),
            pltpu.VMEM((NB * BLOCK,), jnp.float32),
            pltpu.SMEM((1, OWNERS), jnp.int32),
            pltpu.VMEM((SHARD, BLOCK), jnp.bfloat16),
            pltpu.VMEM((SHARD, BLOCK), jnp.bfloat16),
            pltpu.VMEM((2, SHARD, BLOCK), jnp.bfloat16),
            pltpu.VMEM((2, SHARD, BLOCK), jnp.bfloat16),
            pltpu.VMEM((2, SHARD, BLOCK), jnp.bfloat16),
            pltpu.VMEM((4, CHUNK, 768), jnp.bfloat16),
            pltpu.VMEM((STEPS, 768, TILE), jnp.bfloat16),
            pltpu.VMEM((2, NB, 8, BLOCK), jnp.float32),
            pltpu.VMEM((2, OWNERS, 16, BLOCK), jnp.bfloat16),
            pltpu.SMEM((OWNERS,), jnp.int32),
            pltpu.SemaphoreType.DMA((6,)),
            pltpu.SemaphoreType.DMA((STEPS,)),
            pltpu.SemaphoreType.DMA((7,)),
            pltpu.SemaphoreType.DMA((7,)),
            pltpu.SemaphoreType.REGULAR((5, 2)),
            pltpu.SemaphoreType.DMA((2,)),
            pltpu.SemaphoreType.DMA((2,)),
            pltpu.SemaphoreType.DMA((2,)),
        ],
        compiler_params=pltpu.CompilerParams(
            collective_id=0, has_side_effects=True, vmem_limit_bytes=48 * 2**20
        ),
        cost_estimate=pl.CostEstimate(
            flops=8_000_000_000, bytes_accessed=7_000_000, transcendentals=0
        ),
        name="index",
    )(*(
        pltpu.with_memory_space_constraint(x, pltpu.HBM)
        for x in (
            tokens, token_mask, adapter_weight, norm_gain, head_bias, block_counts, head_weight
        )
    ))
    scaled = pl.pallas_call(
        scale_kernel,
        out_shape=jax.ShapeDtypeStruct((2, OWNERS, 2, 8, BLOCK), jnp.float32),
        in_specs=[smem, vmem],
        out_specs=hbm,
        scratch_shapes=[
            pltpu.VMEM((2, 2, OWNERS, 8, BLOCK), jnp.float32),
            pltpu.SemaphoreType.DMA((2, 2)),
        ],
        compiler_params=pltpu.CompilerParams(vmem_limit_bytes=8 * 2**20),
        cost_estimate=pl.CostEstimate(flops=4_000_000, bytes_accessed=800_000, transcendentals=131072),
        name="scale",
    )(block_counts, codes)
    return scaled.reshape(2, OWNERS * 16, BLOCK)


def solution(mesh):
    in_specs = (
        P(("docs", "vocab"), None, None),
        P(("docs", "vocab"), None),
        P(),
        P(),
        P(None, "vocab"),
        P("vocab"),
        P("vocab", None),
    )
    out_specs = P("docs", None, "vocab")
    return jax.shard_map(shards, mesh=mesh, in_specs=in_specs, out_specs=out_specs, check_vma=False)
```

```python
import functools

import jax
import jax.numpy as jnp
from jax import lax
from jax.experimental import pallas as pl
from jax.experimental.pallas import tpu as pltpu
from jax.sharding import PartitionSpec as P

MESH = pl.DeviceIdType.MESH
BLOCK = 128
EPSILON = 1e-05
OWNERS = 32
CHIPS_Y = 4
SIZE_X = 4
SIZE_Z = 8
NB = 30
LEN = 80
SHARD = 2 * LEN
CHUNK = 2 * SHARD
TILE = 768
STEPS = NB * BLOCK // TILE


def index_kernel(
    tok_hbm, mask_hbm, aw_hbm, gain_hbm, bias_hbm, counts_hbm, hw_hbm, recv_ref,
    tok_ref, mask_ref, aw_ref, gain_ref, bias_ref, bias2, counts_ref,
    tok_own, tok_a, tok_b, tok_c, tok_d, hid, wbuf, pooled, pooled_last, send, starts, firsts, order_v, order,
    arg_sem, wsem, order_sem, tok_send, tok_recv, ready, tile_send, tile_recv, tile_own,
):
    d = lax.axis_index("docs")
    v = lax.axis_index("vocab")
    y = v // 2
    c = v % 2
    y1 = y + 1 - 2 * (y % 2)
    y2 = (y + 2) % CHIPS_Y
    y3 = CHIPS_Y - 1 - y
    partners = [y * 2 + 1 - c] + [chip * 2 + core for chip in (y1, y3, y2) for core in (c, 1 - c)]
    x = d // SIZE_Z
    z = d % SIZE_Z

    def across(dx, dz):
        return (x + dx) % SIZE_X * SIZE_Z + (z + dz) % SIZE_Z


    arg_copies = [
        pltpu.make_async_copy(src, dst, arg_sem.at[i])
        for i, (src, dst) in enumerate((
            (tok_hbm, tok_ref), (mask_hbm, mask_ref), (aw_hbm, aw_ref),
            (gain_hbm, gain_ref), (bias_hbm, bias_ref), (counts_hbm, counts_ref),
        ))
    ]
    for copy in arg_copies:
        copy.start()

    barrier = pltpu.get_barrier_semaphore()
    for partner in partners:
        pl.semaphore_signal(barrier, inc=1, device_id=(d, partner), device_id_type=MESH)
    for dx, dz in ((0, 1), (0, -1), (1, 0), (-1, 0)):
        pl.semaphore_signal(barrier, inc=1, device_id=(across(dx, dz), v), device_id_type=MESH)
    for b in range(NB):
        pltpu.make_async_copy(hw_hbm.at[:, b * BLOCK : (b + 1) * BLOCK], wbuf.at[b], wsem).start()

    slot = lax.broadcasted_iota(jnp.int32, (LEN, BLOCK), 0).astype(jnp.float32)
    arg_copies[0].wait()
    arg_copies[1].wait()
    for p in range(2):
        live = jnp.sum(mask_ref[p : p + 1, :].astype(jnp.float32), axis=1, keepdims=True)
        tok = tok_ref[p].astype(jnp.float32)
        tok = jnp.where(slot < live, tok, tok[0:1, :])
        tok_own[p * LEN : (p + 1) * LEN, :] = tok.astype(jnp.bfloat16)

    pl.semaphore_wait(barrier, 11)

    buffers = [None, tok_b, tok_b, tok_c, tok_c, tok_d, tok_d]

    def token_copy(r, core):
        return pltpu.make_async_remote_copy(
            src_ref=tok_own,
            dst_ref=tok_a if r == 0 else buffers[r].at[core],
            send_sem=tok_send.at[r],
            recv_sem=tok_recv.at[r],
            device_id=(d, partners[r]),
            device_id_type=MESH,
        )

    def tokens_in(r):
        token_copy(r, c if r in (1, 3, 5) else 1 - c).wait_recv()

    def tell(r):
        for way, step in enumerate((1, -1)[: 1 if r == 4 else 2]):
            to = across(0, step) if r < 3 else across(step, 0)
            pl.semaphore_signal(ready.at[r, way], inc=1, device_id=(to, v), device_id_type=MESH)

    def told(r):
        for way in range(1 if r == 4 else 2):
            pl.semaphore_wait(ready.at[r, way], 1)

    for r in range(5):
        token_copy(r, c).start()
    tell(0)
    arg_copies[5].wait()

    def note_start(o, at):
        starts[o] = jnp.minimum(at, NB - 1)
        return at + counts_ref[0, o]

    lax.fori_loop(0, OWNERS, note_start, jnp.int32(0))

    def hops(t):
        dx, dz = t
        return min(dx, SIZE_X - dx) + min(dz, SIZE_Z - dz)

    owners = sorted(
        ((dx, dz) for dx in range(SIZE_X) for dz in range(SIZE_Z) if dx or dz), key=hops, reverse=True
    )

    lane = lax.broadcasted_iota(jnp.int32, (8, BLOCK), 1)
    block = jnp.zeros((8, BLOCK), jnp.int32)
    at = jnp.int32(0)
    for r, t in enumerate(owners + [(0, 0)]):
        o = across(*t)
        firsts[r] = jnp.minimum(at, NB - 1)
        block = jnp.where(lane >= at, starts[o] + lane - at, block)
        at = at + counts_ref[0, o]
    order_v[...] = jnp.clip(block, 0, NB - 1)
    order_copy = pltpu.make_async_copy(order_v, order, order_sem)
    order_copy.start()
    pooled_last[...] = jnp.zeros_like(pooled_last)
    for i in (2, 3, 4):
        arg_copies[i].wait()
    for b in range(NB):
        bias2[b] = bias_ref[b * BLOCK : (b + 1) * BLOCK].reshape(1, BLOCK)

    def norm_rows(tok, chunk, at):
        adapted = jnp.dot(tok, aw_ref[...], preferred_element_type=jnp.float32)
        centred = adapted - jnp.mean(adapted, axis=-1, keepdims=True)
        row_var = jnp.mean(centred * centred, axis=-1, keepdims=True)
        normed = centred * lax.rsqrt(row_var + EPSILON) * gain_ref[...].reshape(1, -1)
        hid[chunk, pl.ds(at, tok.shape[0]), :] = normed.astype(jnp.bfloat16)

    def head_step(chunk, i):
        per = TILE // BLOCK
        at = range(i * per, (i + 1) * per)
        if chunk == 3:
            at = [order[0, b] for b in at]
        bias = jnp.concatenate([bias2[b] for b in at], axis=1)
        weights = jnp.concatenate([wbuf[b] for b in at], axis=1)
        logits = jnp.dot(hid[chunk], weights, preferred_element_type=jnp.float32)
        x = jnp.maximum(jnp.max(logits.reshape(4, LEN, TILE), axis=1) + bias, 0.0)
        for _ in range(3):
            x = x * (x + 2.0)
        row = chunk % 2 * 4
        for q in range(per):
            part = x[:, q * BLOCK : (q + 1) * BLOCK]
            if chunk == 3:
                pooled_last[i * per + q, row : row + 4] = part
            else:
                pooled[chunk // 2, i * per + q, row : row + 4] = part

    row8 = lax.broadcasted_iota(jnp.int32, (8, BLOCK), 0)

    def tiles_of(k, o, r):
        at = starts[o]
        two = [pooled[k, at], pooled[k, jnp.minimum(at + 1, NB - 1)]]
        if k == 1:
            at = firsts[r]
            late = [pooled_last[at], pooled_last[jnp.minimum(at + 1, NB - 1)]]
            two = [jnp.where(row8 < 4, a, b) for a, b in zip(two, late)]
        send[k, o] = jnp.concatenate(two, axis=0).astype(jnp.bfloat16)

    def send_tile(k, r):
        o = across(*owners[r])
        tiles_of(k, o, r)
        pltpu.make_async_remote_copy(
            src_ref=send.at[k, o],
            dst_ref=recv_ref.at[k, d],
            send_sem=tile_send.at[k],
            recv_sem=tile_recv.at[k],
            device_id=(o, v),
            device_id_type=MESH,
        ).start()

    def keep_tile(k):
        tiles_of(k, d, OWNERS - 1)
        pltpu.make_async_copy(send.at[k, d], recv_ref.at[k, d], tile_own.at[k]).start()

    def norm_chunk(chunk, buf, piece, pieces):
        rows = CHUNK // pieces
        tok = buf[piece * rows // SHARD, piece * rows % SHARD : piece * rows % SHARD + rows, :]
        norm_rows(tok, chunk, piece * rows)

    for i in range(2):
        norm_rows(tok_own[i * LEN : (i + 1) * LEN], 0, pl.multiple_of(c * SHARD + i * LEN, 16))
    tokens_in(0)
    for r in (5, 6):
        token_copy(r, c).start()
    for i in range(2):
        norm_rows(tok_a[i * LEN : (i + 1) * LEN], 0, pl.multiple_of((1 - c) * SHARD + i * LEN, 16))
    told(0)
    tell(1)
    pltpu.make_async_copy(wbuf, wbuf, wsem).wait()
    for i in range(STEPS - 1):
        head_step(0, i)

    tokens_in(1)
    tokens_in(2)
    told(1)
    tell(2)
    head_step(0, STEPS - 1)
    for i in range(4):
        norm_chunk(1, tok_b, i, 4)
    tokens_in(3)
    tokens_in(4)
    told(2)
    tell(3)
    for i in range(STEPS):
        head_step(1, i)
        if i < 4:
            norm_chunk(2, tok_c, i, 4)
    tokens_in(5)
    tokens_in(6)
    told(3)
    tell(4)
    for i in range(STEPS):
        head_step(2, i)
        if i < 4:
            norm_chunk(3, tok_d, i, 4)
    told(4)

    order_copy.wait()
    for r in range(OWNERS - 1):
        send_tile(0, r)
    keep_tile(0)
    early = TILE // BLOCK // 2
    for i in range(STEPS):
        head_step(3, i)
        for r in range(i * early, min((i + 1) * early, OWNERS - 1)):
            send_tile(1, r)
    for r in range(STEPS * early, OWNERS - 1):
        send_tile(1, r)
    keep_tile(1)

    for r in range(7):
        token_copy(r, c).wait_send()
    for k in range(2):
        pltpu.make_async_copy(send.at[k, d], recv_ref.at[k, d], tile_own.at[k]).wait()
        others = send.at[k, 0 : OWNERS - 1]
        pltpu.make_async_copy(others, others, tile_send.at[k]).wait()
        others = recv_ref.at[k, 0 : OWNERS - 1]
        pltpu.make_async_copy(others, others, tile_recv.at[k]).wait()


def scale_kernel(counts_ref, code_ref, out_hbm, out, sem):
    owner = lax.axis_index("docs")
    y = lax.axis_index("vocab") // 2
    count = counts_ref[0, owner]
    copies = []
    for s in range(2):
        code = code_ref[:, :, s * 8 : (s + 1) * 8, :].astype(jnp.float32)
        top = jnp.max(code.reshape(-1, 8, BLOCK), axis=0)
        top = jnp.max(top, axis=0, keepdims=True)
        peak = jnp.maximum(jnp.log1p(top) * 0.125, 1.0)
        factor = 0.125 / peak
        for h in range(2):
            rows = jnp.log1p(code[h]) * factor
            swapped = jnp.concatenate([rows[:, 4:], rows[:, :4]], axis=1)
            rows = jnp.where(y % 2 == 1 - h, swapped, rows)
            out[s, h] = jnp.where(s < count, rows, 0.0)
            half = y // 2 if h == 0 else 1 - y // 2
            copy = pltpu.make_async_copy(out.at[s, h], out_hbm.at[s, :, half], sem.at[s, h])
            copy.start()
            copies.append(copy)
    for copy in copies:
        copy.wait()


def shards(tokens, token_mask, adapter_weight, norm_gain, head_weight, head_bias, block_counts):
    vmem = pl.BlockSpec(memory_space=pltpu.VMEM)
    smem = pl.BlockSpec(memory_space=pltpu.SMEM)
    hbm = pl.BlockSpec(memory_space=pltpu.HBM)
    codes = pl.pallas_call(
        index_kernel,
        out_shape=jax.ShapeDtypeStruct((2, OWNERS, 16, BLOCK), jnp.bfloat16),
        in_specs=[hbm] * 7,
        out_specs=pl.BlockSpec(memory_space=pl.ANY),
        scratch_shapes=[
            pltpu.VMEM((2, LEN, BLOCK), jnp.bfloat16),
            pltpu.VMEM((2, LEN), jnp.int32),
            pltpu.VMEM((BLOCK, 768), jnp.bfloat16),
            pltpu.VMEM((768,), jnp.float32),
            pltpu.VMEM((NB * BLOCK,), jnp.float32),
            pltpu.VMEM((NB, 1, BLOCK), jnp.float32),
            pltpu.SMEM((1, OWNERS), jnp.int32),
            pltpu.VMEM((SHARD, BLOCK), jnp.bfloat16),
            pltpu.VMEM((SHARD, BLOCK), jnp.bfloat16),
            pltpu.VMEM((2, SHARD, BLOCK), jnp.bfloat16),
            pltpu.VMEM((2, SHARD, BLOCK), jnp.bfloat16),
            pltpu.VMEM((2, SHARD, BLOCK), jnp.bfloat16),
            pltpu.VMEM((4, CHUNK, 768), jnp.bfloat16),
            pltpu.VMEM((NB, 768, BLOCK), jnp.bfloat16),
            pltpu.VMEM((2, NB, 8, BLOCK), jnp.float32),
            pltpu.VMEM((NB, 8, BLOCK), jnp.float32),
            pltpu.VMEM((2, OWNERS, 16, BLOCK), jnp.bfloat16),
            pltpu.SMEM((OWNERS,), jnp.int32),
            pltpu.SMEM((OWNERS,), jnp.int32),
            pltpu.VMEM((8, BLOCK), jnp.int32),
            pltpu.SMEM((8, BLOCK), jnp.int32),
            pltpu.SemaphoreType.DMA((6,)),
            pltpu.SemaphoreType.DMA,
            pltpu.SemaphoreType.DMA,
            pltpu.SemaphoreType.DMA((7,)),
            pltpu.SemaphoreType.DMA((7,)),
            pltpu.SemaphoreType.REGULAR((5, 2)),
            pltpu.SemaphoreType.DMA((2,)),
            pltpu.SemaphoreType.DMA((2,)),
            pltpu.SemaphoreType.DMA((2,)),
        ],
        compiler_params=pltpu.CompilerParams(
            collective_id=0, has_side_effects=True, vmem_limit_bytes=48 * 2**20
        ),
        cost_estimate=pl.CostEstimate(
            flops=8_000_000_000, bytes_accessed=7_000_000, transcendentals=0
        ),
        name="index",
    )(*(
        pltpu.with_memory_space_constraint(x, pltpu.HBM)
        for x in (
            tokens, token_mask, adapter_weight, norm_gain, head_bias, block_counts, head_weight
        )
    ))
    scaled = pl.pallas_call(
        scale_kernel,
        out_shape=jax.ShapeDtypeStruct((2, OWNERS, 2, 8, BLOCK), jnp.float32),
        in_specs=[smem, vmem],
        out_specs=hbm,
        scratch_shapes=[
            pltpu.VMEM((2, 2, OWNERS, 8, BLOCK), jnp.float32),
            pltpu.SemaphoreType.DMA((2, 2)),
        ],
        compiler_params=pltpu.CompilerParams(vmem_limit_bytes=8 * 2**20),
        cost_estimate=pl.CostEstimate(flops=4_000_000, bytes_accessed=800_000, transcendentals=131072),
        name="scale",
    )(block_counts, codes)
    return scaled.reshape(2, OWNERS * 16, BLOCK)


def solution(mesh):
    in_specs = (
        P(("docs", "vocab"), None, None),
        P(("docs", "vocab"), None),
        P(),
        P(),
        P(None, "vocab"),
        P("vocab"),
        P("vocab", None),
    )
    out_specs = P("docs", None, "vocab")
    return jax.shard_map(shards, mesh=mesh, in_specs=in_specs, out_specs=out_specs, check_vma=False)
```

```python
import functools

import jax
import jax.numpy as jnp
from jax import lax
from jax.experimental import pallas as pl
from jax.experimental.pallas import tpu as pltpu
from jax.sharding import PartitionSpec as P

MESH = pl.DeviceIdType.MESH
BLOCK = 128
EPSILON = 1e-05
OWNERS = 32
CHIPS_Y = 4
SIZE_X = 4
SIZE_Z = 8
NB = 30
LEN = 80
SHARD = 2 * LEN
CHUNK = 2 * SHARD
TILE = 768
STEPS = NB * BLOCK // TILE


def index_kernel(
    tok_hbm, mask_hbm, aw_hbm, gain_hbm, bias_hbm, counts_hbm, hw_hbm, out_ref,
    tok_ref, mask_ref, aw_ref, gain_ref, bias_ref, bias2, counts_ref,
    tok_own, tok_a, tok_b, tok_c, tok_d, hid, wbuf, pooled, pooled_last, send, recv_ref, impact, starts, firsts, order_v, order,
    arg_sem, wsem, order_sem, tok_send, tok_recv, ready, tile_send, tile_recv, tile_own,
):
    d = lax.axis_index("docs")
    v = lax.axis_index("vocab")
    y = v // 2
    c = v % 2
    y1 = y + 1 - 2 * (y % 2)
    y2 = (y + 2) % CHIPS_Y
    y3 = CHIPS_Y - 1 - y
    partners = [y * 2 + 1 - c] + [chip * 2 + core for chip in (y1, y3, y2) for core in (c, 1 - c)]
    x = d // SIZE_Z
    z = d % SIZE_Z

    def across(dx, dz):
        return (x + dx) % SIZE_X * SIZE_Z + (z + dz) % SIZE_Z


    arg_copies = [
        pltpu.make_async_copy(src, dst, arg_sem.at[i])
        for i, (src, dst) in enumerate((
            (tok_hbm, tok_ref), (mask_hbm, mask_ref), (aw_hbm, aw_ref),
            (gain_hbm, gain_ref), (bias_hbm, bias_ref), (counts_hbm, counts_ref),
        ))
    ]
    for copy in arg_copies:
        copy.start()

    barrier = pltpu.get_barrier_semaphore()
    for partner in partners:
        pl.semaphore_signal(barrier, inc=1, device_id=(d, partner), device_id_type=MESH)
    for dx, dz in ((0, 1), (0, -1), (1, 0), (-1, 0)):
        pl.semaphore_signal(barrier, inc=1, device_id=(across(dx, dz), v), device_id_type=MESH)
    for b in range(NB):
        pltpu.make_async_copy(hw_hbm.at[:, b * BLOCK : (b + 1) * BLOCK], wbuf.at[b], wsem).start()

    slot = lax.broadcasted_iota(jnp.int32, (LEN, BLOCK), 0).astype(jnp.float32)
    arg_copies[0].wait()
    arg_copies[1].wait()
    for p in range(2):
        live = jnp.sum(mask_ref[p : p + 1, :].astype(jnp.float32), axis=1, keepdims=True)
        tok = tok_ref[p].astype(jnp.float32)
        tok = jnp.where(slot < live, tok, tok[0:1, :])
        tok_own[p * LEN : (p + 1) * LEN, :] = tok.astype(jnp.bfloat16)

    pl.semaphore_wait(barrier, 11)

    buffers = [None, tok_b, tok_b, tok_c, tok_c, tok_d, tok_d]

    def token_copy(r, core):
        return pltpu.make_async_remote_copy(
            src_ref=tok_own,
            dst_ref=tok_a if r == 0 else buffers[r].at[core],
            send_sem=tok_send.at[r],
            recv_sem=tok_recv.at[r],
            device_id=(d, partners[r]),
            device_id_type=MESH,
        )

    def tokens_in(r):
        token_copy(r, c if r in (1, 3, 5) else 1 - c).wait_recv()

    def tell(r):
        for way, step in enumerate((1, -1)[: 1 if r == 4 else 2]):
            to = across(0, step) if r < 3 else across(step, 0)
            pl.semaphore_signal(ready.at[r, way], inc=1, device_id=(to, v), device_id_type=MESH)

    def told(r):
        for way in range(1 if r == 4 else 2):
            pl.semaphore_wait(ready.at[r, way], 1)

    for r in range(5):
        token_copy(r, c).start()
    tell(0)
    arg_copies[5].wait()

    def note_start(o, at):
        starts[o] = jnp.minimum(at, NB - 1)
        return at + counts_ref[0, o]

    lax.fori_loop(0, OWNERS, note_start, jnp.int32(0))

    def hops(t):
        dx, dz = t
        return min(dx, SIZE_X - dx) + min(dz, SIZE_Z - dz)

    owners = sorted(
        ((dx, dz) for dx in range(SIZE_X) for dz in range(SIZE_Z) if dx or dz), key=hops, reverse=True
    )

    lane = lax.broadcasted_iota(jnp.int32, (8, BLOCK), 1)
    block = jnp.zeros((8, BLOCK), jnp.int32)
    at = jnp.int32(0)
    for r, t in enumerate(owners + [(0, 0)]):
        o = across(*t)
        firsts[r] = jnp.minimum(at, NB - 1)
        block = jnp.where(lane >= at, starts[o] + lane - at, block)
        at = at + counts_ref[0, o]
    order_v[...] = jnp.clip(block, 0, NB - 1)
    order_copy = pltpu.make_async_copy(order_v, order, order_sem)
    order_copy.start()
    pooled_last[...] = jnp.zeros_like(pooled_last)
    for i in (2, 3, 4):
        arg_copies[i].wait()
    for b in range(NB):
        bias2[b] = bias_ref[b * BLOCK : (b + 1) * BLOCK].reshape(1, BLOCK)

    def norm_rows(tok, chunk, at):
        adapted = jnp.dot(tok, aw_ref[...], preferred_element_type=jnp.float32)
        centred = adapted - jnp.mean(adapted, axis=-1, keepdims=True)
        row_var = jnp.mean(centred * centred, axis=-1, keepdims=True)
        normed = centred * lax.rsqrt(row_var + EPSILON) * gain_ref[...].reshape(1, -1)
        hid[chunk, pl.ds(at, tok.shape[0]), :] = normed.astype(jnp.bfloat16)

    def head_step(chunk, i):
        per = TILE // BLOCK
        at = range(i * per, (i + 1) * per)
        if chunk == 3:
            at = [order[0, b] for b in at]
        bias = jnp.concatenate([bias2[b] for b in at], axis=1)
        weights = jnp.concatenate([wbuf[b] for b in at], axis=1)
        logits = jnp.dot(hid[chunk], weights, preferred_element_type=jnp.float32)
        x = jnp.maximum(jnp.max(logits.reshape(4, LEN, TILE), axis=1) + bias, 0.0)
        for _ in range(3):
            x = x * (x + 2.0)
        row = chunk % 2 * 4
        for q in range(per):
            part = x[:, q * BLOCK : (q + 1) * BLOCK]
            if chunk == 3:
                pooled_last[i * per + q, row : row + 4] = part
            else:
                pooled[chunk // 2, i * per + q, row : row + 4] = part

    row8 = lax.broadcasted_iota(jnp.int32, (8, BLOCK), 0)

    def tiles_of(k, o, r):
        at = starts[o]
        two = [pooled[k, at], pooled[k, jnp.minimum(at + 1, NB - 1)]]
        if k == 1:
            at = firsts[r]
            late = [pooled_last[at], pooled_last[jnp.minimum(at + 1, NB - 1)]]
            two = [jnp.where(row8 < 4, a, b) for a, b in zip(two, late)]
        send[k, o] = jnp.concatenate(two, axis=0).astype(jnp.bfloat16)

    def send_tile(k, r):
        o = across(*owners[r])
        tiles_of(k, o, r)
        pltpu.make_async_remote_copy(
            src_ref=send.at[k, o],
            dst_ref=recv_ref.at[k, d],
            send_sem=tile_send.at[k],
            recv_sem=tile_recv.at[k],
            device_id=(o, v),
            device_id_type=MESH,
        ).start()

    def keep_tile(k):
        tiles_of(k, d, OWNERS - 1)
        pltpu.make_async_copy(send.at[k, d], recv_ref.at[k, d], tile_own.at[k]).start()

    def norm_chunk(chunk, buf, piece, pieces):
        rows = CHUNK // pieces
        tok = buf[piece * rows // SHARD, piece * rows % SHARD : piece * rows % SHARD + rows, :]
        norm_rows(tok, chunk, piece * rows)

    for i in range(2):
        norm_rows(tok_own[i * LEN : (i + 1) * LEN], 0, pl.multiple_of(c * SHARD + i * LEN, 16))
    tokens_in(0)
    for r in (5, 6):
        token_copy(r, c).start()
    for i in range(2):
        norm_rows(tok_a[i * LEN : (i + 1) * LEN], 0, pl.multiple_of((1 - c) * SHARD + i * LEN, 16))
    told(0)
    tell(1)
    pltpu.make_async_copy(wbuf, wbuf, wsem).wait()
    for i in range(STEPS - 1):
        head_step(0, i)

    tokens_in(1)
    tokens_in(2)
    told(1)
    tell(2)
    head_step(0, STEPS - 1)
    for i in range(4):
        norm_chunk(1, tok_b, i, 4)
    tokens_in(3)
    tokens_in(4)
    told(2)
    tell(3)
    for i in range(STEPS):
        head_step(1, i)
        if i < 4:
            norm_chunk(2, tok_c, i, 4)
    tokens_in(5)
    tokens_in(6)
    told(3)
    tell(4)
    for i in range(STEPS):
        head_step(2, i)
        if i < 4:
            norm_chunk(3, tok_d, i, 4)
    told(4)

    order_copy.wait()
    for r in range(OWNERS - 1):
        send_tile(0, r)
    keep_tile(0)
    early = TILE // BLOCK // 2
    for i in range(STEPS):
        head_step(3, i)
        for r in range(i * early, min((i + 1) * early, OWNERS - 1)):
            send_tile(1, r)
    for r in range(STEPS * early, OWNERS - 1):
        send_tile(1, r)
    keep_tile(1)

    def tiles_in(k):
        pltpu.make_async_copy(send.at[k, d], recv_ref.at[k, d], tile_own.at[k]).wait()
        others = recv_ref.at[k, 0 : OWNERS - 1]
        pltpu.make_async_copy(others, others, tile_recv.at[k]).wait()

    def codes(k, s):
        return recv_ref[k, :, s * 8 : (s + 1) * 8, :].astype(jnp.float32)

    def in_order(k, rows):
        return jnp.where(y % 2 == 1 - k, jnp.concatenate([rows[:, 4:], rows[:, :4]], axis=1), rows)

    tiles_in(0)
    tops = []
    for s in range(2):
        code = codes(0, s)
        tops.append(jnp.max(code, axis=0))
        impact[s] = in_order(0, jnp.log1p(code))
    for r in range(7):
        token_copy(r, c).wait_send()
    sent = send.at[0, 0 : OWNERS - 1]
    pltpu.make_async_copy(sent, sent, tile_send.at[0]).wait()

    tiles_in(1)
    count = jnp.full((8, BLOCK), counts_ref[0, d])
    for s in range(2):
        code = codes(1, s)
        top = jnp.max(jnp.maximum(tops[s], jnp.max(code, axis=0)), axis=0, keepdims=True)
        factor = 0.125 / jnp.maximum(jnp.log1p(top) * 0.125, 1.0)
        out_ref[s, :, y // 2] = jnp.where(count > s, impact[s] * factor, 0.0)
        out_ref[s, :, 1 - y // 2] = jnp.where(count > s, in_order(1, jnp.log1p(code)) * factor, 0.0)
    sent = send.at[1, 0 : OWNERS - 1]
    pltpu.make_async_copy(sent, sent, tile_send.at[1]).wait()


def shards(tokens, token_mask, adapter_weight, norm_gain, head_weight, head_bias, block_counts):
    hbm = pl.BlockSpec(memory_space=pltpu.HBM)
    scaled = pl.pallas_call(
        index_kernel,
        out_shape=jax.ShapeDtypeStruct((2, OWNERS, 2, 8, BLOCK), jnp.float32),
        in_specs=[hbm] * 7,
        out_specs=pl.BlockSpec(memory_space=pltpu.VMEM),
        scratch_shapes=[
            pltpu.VMEM((2, LEN, BLOCK), jnp.bfloat16),
            pltpu.VMEM((2, LEN), jnp.int32),
            pltpu.VMEM((BLOCK, 768), jnp.bfloat16),
            pltpu.VMEM((768,), jnp.float32),
            pltpu.VMEM((NB * BLOCK,), jnp.float32),
            pltpu.VMEM((NB, 1, BLOCK), jnp.float32),
            pltpu.SMEM((1, OWNERS), jnp.int32),
            pltpu.VMEM((SHARD, BLOCK), jnp.bfloat16),
            pltpu.VMEM((SHARD, BLOCK), jnp.bfloat16),
            pltpu.VMEM((2, SHARD, BLOCK), jnp.bfloat16),
            pltpu.VMEM((2, SHARD, BLOCK), jnp.bfloat16),
            pltpu.VMEM((2, SHARD, BLOCK), jnp.bfloat16),
            pltpu.VMEM((4, CHUNK, 768), jnp.bfloat16),
            pltpu.VMEM((NB, 768, BLOCK), jnp.bfloat16),
            pltpu.VMEM((2, NB, 8, BLOCK), jnp.float32),
            pltpu.VMEM((NB, 8, BLOCK), jnp.float32),
            pltpu.VMEM((2, OWNERS, 16, BLOCK), jnp.bfloat16),
            pltpu.VMEM((2, OWNERS, 16, BLOCK), jnp.bfloat16),
            pltpu.VMEM((2, OWNERS, 8, BLOCK), jnp.float32),
            pltpu.SMEM((OWNERS,), jnp.int32),
            pltpu.SMEM((OWNERS,), jnp.int32),
            pltpu.VMEM((8, BLOCK), jnp.int32),
            pltpu.SMEM((8, BLOCK), jnp.int32),
            pltpu.SemaphoreType.DMA((6,)),
            pltpu.SemaphoreType.DMA,
            pltpu.SemaphoreType.DMA,
            pltpu.SemaphoreType.DMA((7,)),
            pltpu.SemaphoreType.DMA((7,)),
            pltpu.SemaphoreType.REGULAR((5, 2)),
            pltpu.SemaphoreType.DMA((2,)),
            pltpu.SemaphoreType.DMA((2,)),
            pltpu.SemaphoreType.DMA((2,)),
        ],
        compiler_params=pltpu.CompilerParams(
            collective_id=0, has_side_effects=True, vmem_limit_bytes=48 * 2**20
        ),
        cost_estimate=pl.CostEstimate(
            flops=8_000_000_000, bytes_accessed=7_000_000, transcendentals=0
        ),
        name="index",
    )(*(
        pltpu.with_memory_space_constraint(x, pltpu.HBM)
        for x in (
            tokens, token_mask, adapter_weight, norm_gain, head_bias, block_counts, head_weight
        )
    ))
    return scaled.reshape(2, OWNERS * 16, BLOCK)


def solution(mesh):
    in_specs = (
        P(("docs", "vocab"), None, None),
        P(("docs", "vocab"), None),
        P(),
        P(),
        P(None, "vocab"),
        P("vocab"),
        P("vocab", None),
    )
    out_specs = P("docs", None, "vocab")
    return jax.shard_map(shards, mesh=mesh, in_specs=in_specs, out_specs=out_specs, check_vma=False)
```

```python
import functools

import jax
import jax.numpy as jnp
from jax import lax
from jax.experimental import pallas as pl
from jax.experimental.pallas import tpu as pltpu
from jax.sharding import PartitionSpec as P

MESH = pl.DeviceIdType.MESH
BLOCK = 128
EPSILON = 1e-05
OWNERS = 32
CHIPS_Y = 4
SIZE_X = 4
SIZE_Z = 8
NB = 30
LEN = 80
SHARD = 2 * LEN
CHUNK = 2 * SHARD
TILE = 768
STEPS = NB * BLOCK // TILE


def index_kernel(
    tok_hbm, mask_hbm, aw_hbm, gain_hbm, bias_hbm, counts_hbm, hw_hbm, out_ref,
    tok_ref, mask_ref, aw_ref, gain_ref, bias_ref, bias2, counts_ref,
    tok_own, tok_a, tok_b0, tok_b1, tok_c, tok_d, hid, wbuf, pooled, pooled_last, send, recv_ref, impact, starts, firsts, order_v, order,
    arg_sem, wsem, order_sem, tok_send, tok_recv, ready, tile_send, tile_recv, tile_own,
):
    d = lax.axis_index("docs")
    v = lax.axis_index("vocab")
    y = v // 2
    c = v % 2
    y1 = y + 1 - 2 * (y % 2)
    y2 = (y + 2) % CHIPS_Y
    y3 = CHIPS_Y - 1 - y
    partners = [y * 2 + 1 - c] + [chip * 2 + core for chip in (y1, y3, y2) for core in (c, 1 - c)]
    x = d // SIZE_Z
    z = d % SIZE_Z

    def across(dx, dz):
        return (x + dx) % SIZE_X * SIZE_Z + (z + dz) % SIZE_Z


    arg_copies = [
        pltpu.make_async_copy(src, dst, arg_sem.at[i])
        for i, (src, dst) in enumerate((
            (tok_hbm, tok_ref), (mask_hbm, mask_ref), (aw_hbm, aw_ref),
            (gain_hbm, gain_ref), (bias_hbm, bias_ref), (counts_hbm, counts_ref),
        ))
    ]
    for copy in arg_copies:
        copy.start()

    barrier = pltpu.get_barrier_semaphore()
    for partner in partners:
        pl.semaphore_signal(barrier, inc=1, device_id=(d, partner), device_id_type=MESH)
    for dx, dz in ((0, 1), (0, -1), (1, 0), (-1, 0)):
        pl.semaphore_signal(barrier, inc=1, device_id=(across(dx, dz), v), device_id_type=MESH)
    for b in range(NB):
        pltpu.make_async_copy(hw_hbm.at[:, b * BLOCK : (b + 1) * BLOCK], wbuf.at[b], wsem).start()

    slot = lax.broadcasted_iota(jnp.int32, (LEN, BLOCK), 0).astype(jnp.float32)
    arg_copies[0].wait()
    arg_copies[1].wait()
    for p in range(2):
        live = jnp.sum(mask_ref[p : p + 1, :].astype(jnp.float32), axis=1, keepdims=True)
        tok = tok_ref[p].astype(jnp.float32)
        tok = jnp.where(slot < live, tok, tok[0:1, :])
        tok_own[p * LEN : (p + 1) * LEN, :] = tok.astype(jnp.bfloat16)

    pl.semaphore_wait(barrier, 11)

    buffers = [tok_a, tok_b0, tok_b1, tok_c, tok_c, tok_d, tok_d]

    def token_copy(r, core):
        return pltpu.make_async_remote_copy(
            src_ref=tok_own,
            dst_ref=buffers[r] if r < 3 else buffers[r].at[core],
            send_sem=tok_send.at[r],
            recv_sem=tok_recv.at[r],
            device_id=(d, partners[r]),
            device_id_type=MESH,
        )

    def tokens_in(r):
        token_copy(r, c if r in (1, 3, 5) else 1 - c).wait_recv()

    def tell(r):
        for way, step in enumerate((1, -1)[: 1 if r == 4 else 2]):
            to = across(0, step) if r < 3 else across(step, 0)
            pl.semaphore_signal(ready.at[r, way], inc=1, device_id=(to, v), device_id_type=MESH)

    def told(r):
        for way in range(1 if r == 4 else 2):
            pl.semaphore_wait(ready.at[r, way], 1)

    for r in range(5):
        token_copy(r, c).start()
    tell(0)
    arg_copies[5].wait()

    def note_start(o, at):
        starts[o] = jnp.minimum(at, NB - 1)
        return at + counts_ref[0, o]

    lax.fori_loop(0, OWNERS, note_start, jnp.int32(0))

    def hops(t):
        dx, dz = t
        return min(dx, SIZE_X - dx) + min(dz, SIZE_Z - dz)

    owners = sorted(
        ((dx, dz) for dx in range(SIZE_X) for dz in range(SIZE_Z) if dx or dz), key=hops, reverse=True
    )

    lane = lax.broadcasted_iota(jnp.int32, (8, BLOCK), 1)
    block = jnp.zeros((8, BLOCK), jnp.int32)
    at = jnp.int32(0)
    for r, t in enumerate(owners + [(0, 0)]):
        o = across(*t)
        firsts[r] = jnp.minimum(at, NB - 1)
        block = jnp.where(lane >= at, starts[o] + lane - at, block)
        at = at + counts_ref[0, o]
    order_v[...] = jnp.clip(block, 0, NB - 1)
    order_copy = pltpu.make_async_copy(order_v, order, order_sem)
    order_copy.start()
    pooled_last[...] = jnp.zeros_like(pooled_last)
    for i in (2, 3, 4):
        arg_copies[i].wait()
    for b in range(NB):
        bias2[b] = bias_ref[b * BLOCK : (b + 1) * BLOCK].reshape(1, BLOCK)

    def norm_rows(tok, chunk, at):
        adapted = jnp.dot(tok, aw_ref[...], preferred_element_type=jnp.float32)
        centred = adapted - jnp.mean(adapted, axis=-1, keepdims=True)
        row_var = jnp.mean(centred * centred, axis=-1, keepdims=True)
        normed = centred * lax.rsqrt(row_var + EPSILON) * gain_ref[...].reshape(1, -1)
        hid[chunk, pl.ds(at, tok.shape[0]), :] = normed.astype(jnp.bfloat16)

    def head_step(chunk, i):
        per = TILE // BLOCK
        at = range(i * per, (i + 1) * per)
        if chunk == 3:
            at = [order[0, b] for b in at]
        bias = jnp.concatenate([bias2[b] for b in at], axis=1)
        weights = jnp.concatenate([wbuf[b] for b in at], axis=1)
        logits = jnp.dot(hid[chunk], weights, preferred_element_type=jnp.float32)
        x = jnp.maximum(jnp.max(logits.reshape(4, LEN, TILE), axis=1) + bias, 0.0)
        for _ in range(3):
            x = x * (x + 2.0)
        row = chunk % 2 * 4
        for q in range(per):
            part = x[:, q * BLOCK : (q + 1) * BLOCK]
            if chunk == 3:
                pooled_last[i * per + q, row : row + 4] = part
            else:
                pooled[chunk // 2, i * per + q, row : row + 4] = part

    row8 = lax.broadcasted_iota(jnp.int32, (8, BLOCK), 0)

    def tiles_of(k, o, r):
        at = starts[o]
        two = [pooled[k, at], pooled[k, jnp.minimum(at + 1, NB - 1)]]
        if k == 1:
            at = firsts[r]
            late = [pooled_last[at], pooled_last[jnp.minimum(at + 1, NB - 1)]]
            two = [jnp.where(row8 < 4, a, b) for a, b in zip(two, late)]
        send[k, o] = jnp.concatenate(two, axis=0).astype(jnp.bfloat16)

    def send_tile(k, r):
        o = across(*owners[r])
        tiles_of(k, o, r)
        pltpu.make_async_remote_copy(
            src_ref=send.at[k, o],
            dst_ref=recv_ref.at[k, d],
            send_sem=tile_send.at[k],
            recv_sem=tile_recv.at[k],
            device_id=(o, v),
            device_id_type=MESH,
        ).start()

    def keep_tile(k):
        tiles_of(k, d, OWNERS - 1)
        pltpu.make_async_copy(send.at[k, d], recv_ref.at[k, d], tile_own.at[k]).start()

    def norm_chunk(chunk, buf, piece, pieces):
        rows = CHUNK // pieces
        tok = buf[piece * rows // SHARD, piece * rows % SHARD : piece * rows % SHARD + rows, :]
        norm_rows(tok, chunk, piece * rows)

    for i in range(2):
        norm_rows(tok_own[i * LEN : (i + 1) * LEN], 0, pl.multiple_of(c * SHARD + i * LEN, 16))
    tokens_in(0)
    for r in (5, 6):
        token_copy(r, c).start()
    for i in range(2):
        norm_rows(tok_a[i * LEN : (i + 1) * LEN], 0, pl.multiple_of((1 - c) * SHARD + i * LEN, 16))
    told(0)
    tell(1)
    pltpu.make_async_copy(wbuf, wbuf, wsem).wait()
    for i in range(STEPS - 1):
        head_step(0, i)

    def norm_near(buf, core):
        for i in range(2):
            norm_rows(buf[i * LEN : (i + 1) * LEN], 1, pl.multiple_of(core * SHARD + i * LEN, 16))

    told(1)
    tell(2)
    tokens_in(1)
    head_step(0, STEPS - 1)
    norm_near(tok_b0, c)
    tokens_in(2)
    norm_near(tok_b1, 1 - c)
    tokens_in(3)
    tokens_in(4)
    told(2)
    tell(3)
    for i in range(STEPS):
        head_step(1, i)
        if i < 4:
            norm_chunk(2, tok_c, i, 4)
    tokens_in(5)
    tokens_in(6)
    told(3)
    tell(4)
    for i in range(STEPS):
        head_step(2, i)
        if i < 4:
            norm_chunk(3, tok_d, i, 4)
    told(4)

    order_copy.wait()
    for r in range(OWNERS - 1):
        send_tile(0, r)
    keep_tile(0)
    early = TILE // BLOCK // 2
    for i in range(STEPS):
        head_step(3, i)
        if i % 2:
            for r in range((i - 1) * early, min((i + 1) * early, OWNERS - 1)):
                send_tile(1, r)
    for r in range((STEPS - 1) * early, OWNERS - 1):
        send_tile(1, r)
    keep_tile(1)

    def tiles_in(k):
        pltpu.make_async_copy(send.at[k, d], recv_ref.at[k, d], tile_own.at[k]).wait()
        others = recv_ref.at[k, 0 : OWNERS - 1]
        pltpu.make_async_copy(others, others, tile_recv.at[k]).wait()

    def codes(k, s):
        return recv_ref[k, :, s * 8 : (s + 1) * 8, :].astype(jnp.float32)

    def in_order(k, rows):
        return jnp.where(y % 2 == 1 - k, jnp.concatenate([rows[:, 4:], rows[:, :4]], axis=1), rows)

    tiles_in(0)
    tops = []
    for s in range(2):
        code = codes(0, s)
        tops.append(jnp.max(code, axis=0))
        impact[s] = in_order(0, jnp.log1p(code))
    for r in range(7):
        token_copy(r, c).wait_send()
    sent = send.at[0, 0 : OWNERS - 1]
    pltpu.make_async_copy(sent, sent, tile_send.at[0]).wait()

    tiles_in(1)
    count = jnp.full((8, BLOCK), counts_ref[0, d])
    for s in range(2):
        code = codes(1, s)
        top = jnp.max(jnp.maximum(tops[s], jnp.max(code, axis=0)), axis=0, keepdims=True)
        factor = 0.125 / jnp.maximum(jnp.log1p(top) * 0.125, 1.0)
        out_ref[s, :, y // 2] = jnp.where(count > s, impact[s] * factor, 0.0)
        out_ref[s, :, 1 - y // 2] = jnp.where(count > s, in_order(1, jnp.log1p(code)) * factor, 0.0)
    sent = send.at[1, 0 : OWNERS - 1]
    pltpu.make_async_copy(sent, sent, tile_send.at[1]).wait()


def shards(tokens, token_mask, adapter_weight, norm_gain, head_weight, head_bias, block_counts):
    hbm = pl.BlockSpec(memory_space=pltpu.HBM)
    scaled = pl.pallas_call(
        index_kernel,
        out_shape=jax.ShapeDtypeStruct((2, OWNERS, 2, 8, BLOCK), jnp.float32),
        in_specs=[hbm] * 7,
        out_specs=pl.BlockSpec(memory_space=pltpu.VMEM),
        scratch_shapes=[
            pltpu.VMEM((2, LEN, BLOCK), jnp.bfloat16),
            pltpu.VMEM((2, LEN), jnp.int32),
            pltpu.VMEM((BLOCK, 768), jnp.bfloat16),
            pltpu.VMEM((768,), jnp.float32),
            pltpu.VMEM((NB * BLOCK,), jnp.float32),
            pltpu.VMEM((NB, 1, BLOCK), jnp.float32),
            pltpu.SMEM((1, OWNERS), jnp.int32),
            pltpu.VMEM((SHARD, BLOCK), jnp.bfloat16),
            pltpu.VMEM((SHARD, BLOCK), jnp.bfloat16),
            pltpu.VMEM((SHARD, BLOCK), jnp.bfloat16),
            pltpu.VMEM((SHARD, BLOCK), jnp.bfloat16),
            pltpu.VMEM((2, SHARD, BLOCK), jnp.bfloat16),
            pltpu.VMEM((2, SHARD, BLOCK), jnp.bfloat16),
            pltpu.VMEM((4, CHUNK, 768), jnp.bfloat16),
            pltpu.VMEM((NB, 768, BLOCK), jnp.bfloat16),
            pltpu.VMEM((2, NB, 8, BLOCK), jnp.float32),
            pltpu.VMEM((NB, 8, BLOCK), jnp.float32),
            pltpu.VMEM((2, OWNERS, 16, BLOCK), jnp.bfloat16),
            pltpu.VMEM((2, OWNERS, 16, BLOCK), jnp.bfloat16),
            pltpu.VMEM((2, OWNERS, 8, BLOCK), jnp.float32),
            pltpu.SMEM((OWNERS,), jnp.int32),
            pltpu.SMEM((OWNERS,), jnp.int32),
            pltpu.VMEM((8, BLOCK), jnp.int32),
            pltpu.SMEM((8, BLOCK), jnp.int32),
            pltpu.SemaphoreType.DMA((6,)),
            pltpu.SemaphoreType.DMA,
            pltpu.SemaphoreType.DMA,
            pltpu.SemaphoreType.DMA((7,)),
            pltpu.SemaphoreType.DMA((7,)),
            pltpu.SemaphoreType.REGULAR((5, 2)),
            pltpu.SemaphoreType.DMA((2,)),
            pltpu.SemaphoreType.DMA((2,)),
            pltpu.SemaphoreType.DMA((2,)),
        ],
        compiler_params=pltpu.CompilerParams(
            collective_id=0, has_side_effects=True, vmem_limit_bytes=48 * 2**20
        ),
        cost_estimate=pl.CostEstimate(
            flops=8_000_000_000, bytes_accessed=7_000_000, transcendentals=0
        ),
        name="index",
    )(*(
        pltpu.with_memory_space_constraint(x, pltpu.HBM)
        for x in (
            tokens, token_mask, adapter_weight, norm_gain, head_bias, block_counts, head_weight
        )
    ))
    return scaled.reshape(2, OWNERS * 16, BLOCK)


def solution(mesh):
    in_specs = (
        P(("docs", "vocab"), None, None),
        P(("docs", "vocab"), None),
        P(),
        P(),
        P(None, "vocab"),
        P("vocab"),
        P("vocab", None),
    )
    out_specs = P("docs", None, "vocab")
    return jax.shard_map(shards, mesh=mesh, in_specs=in_specs, out_specs=out_specs, check_vma=False)
```

```python
import functools

import jax
import jax.numpy as jnp
from jax import lax
from jax.experimental import pallas as pl
from jax.experimental.pallas import tpu as pltpu
from jax.sharding import PartitionSpec as P

MESH = pl.DeviceIdType.MESH
BLOCK = 128
EPSILON = 1e-05
OWNERS = 32
CHIPS_Y = 4
SIZE_X = 4
SIZE_Z = 8
NB = 30
LEN = 80
SHARD = 2 * LEN
CHUNK = 2 * SHARD
TILE = 768
STEPS = NB * BLOCK // TILE


def index_kernel(
    tok_hbm, mask_hbm, aw_hbm, gain_hbm, bias_hbm, counts_hbm, hw_hbm, out_ref,
    tok_ref, mask_ref, aw_ref, gain_ref, bias_ref, bias2, counts_ref,
    tok_own, tok_a, tok_b0, tok_b1, tok_c, tok_d, hid, wbuf, pooled, pooled_last, send, recv_ref, impact, starts, firsts, order_v, order,
    arg_sem, wsem, order_sem, tok_send, tok_recv, ready, tile_send, tile_recv, tile_own,
):
    d = lax.axis_index("docs")
    v = lax.axis_index("vocab")
    y = v // 2
    c = v % 2
    y1 = y + 1 - 2 * (y % 2)
    y2 = (y + 2) % CHIPS_Y
    y3 = CHIPS_Y - 1 - y
    partners = [y * 2 + 1 - c] + [chip * 2 + core for chip in (y1, y3, y2) for core in (c, 1 - c)]
    x = d // SIZE_Z
    z = d % SIZE_Z

    def across(dx, dz):
        return (x + dx) % SIZE_X * SIZE_Z + (z + dz) % SIZE_Z


    arg_copies = [
        pltpu.make_async_copy(src, dst, arg_sem.at[i])
        for i, (src, dst) in enumerate((
            (tok_hbm, tok_ref), (mask_hbm, mask_ref), (aw_hbm, aw_ref),
            (gain_hbm, gain_ref), (bias_hbm, bias_ref), (counts_hbm, counts_ref),
        ))
    ]
    for copy in arg_copies:
        copy.start()

    barrier = pltpu.get_barrier_semaphore()
    for partner in partners:
        pl.semaphore_signal(barrier, inc=1, device_id=(d, partner), device_id_type=MESH)
    for dx, dz in ((0, 1), (0, -1), (1, 0), (-1, 0)):
        pl.semaphore_signal(barrier, inc=1, device_id=(across(dx, dz), v), device_id_type=MESH)
    for b in range(NB):
        pltpu.make_async_copy(hw_hbm.at[:, b * BLOCK : (b + 1) * BLOCK], wbuf.at[b], wsem).start()

    slot = lax.broadcasted_iota(jnp.int32, (LEN, BLOCK), 0).astype(jnp.float32)
    arg_copies[0].wait()
    arg_copies[1].wait()
    for p in range(2):
        live = jnp.sum(mask_ref[p : p + 1, :].astype(jnp.float32), axis=1, keepdims=True)
        tok = tok_ref[p].astype(jnp.float32)
        tok = jnp.where(slot < live, tok, tok[0:1, :])
        tok_own[p * LEN : (p + 1) * LEN, :] = tok.astype(jnp.bfloat16)

    pl.semaphore_wait(barrier, 11)

    buffers = [tok_a, tok_b0, tok_b1, tok_c, tok_c, tok_d, tok_d]

    def token_copy(r, core):
        return pltpu.make_async_remote_copy(
            src_ref=tok_own,
            dst_ref=buffers[r] if r < 3 else buffers[r].at[core],
            send_sem=tok_send.at[r],
            recv_sem=tok_recv.at[r],
            device_id=(d, partners[r]),
            device_id_type=MESH,
        )

    def tokens_in(r):
        token_copy(r, c if r in (1, 3, 5) else 1 - c).wait_recv()

    def tell(r):
        for way, step in enumerate((1, -1)[: 1 if r == 4 else 2]):
            to = across(0, step) if r < 3 else across(step, 0)
            pl.semaphore_signal(ready.at[r, way], inc=1, device_id=(to, v), device_id_type=MESH)

    def told(r):
        for way in range(1 if r == 4 else 2):
            pl.semaphore_wait(ready.at[r, way], 1)

    for r in range(5):
        token_copy(r, c).start()
    tell(0)
    arg_copies[5].wait()

    def note_start(o, at):
        starts[o] = jnp.minimum(at, NB - 1)
        return at + counts_ref[0, o]

    lax.fori_loop(0, OWNERS, note_start, jnp.int32(0))

    def hops(t):
        dx, dz = t
        return min(dx, SIZE_X - dx) + min(dz, SIZE_Z - dz)

    owners = sorted(
        ((dx, dz) for dx in range(SIZE_X) for dz in range(SIZE_Z) if dx or dz), key=hops, reverse=True
    )

    lane = lax.broadcasted_iota(jnp.int32, (8, BLOCK), 1)
    block = jnp.zeros((8, BLOCK), jnp.int32)
    at = jnp.int32(0)
    for r, t in enumerate(owners + [(0, 0)]):
        o = across(*t)
        firsts[r] = jnp.minimum(at, NB - 1)
        block = jnp.where(lane >= at, starts[o] + lane - at, block)
        at = at + counts_ref[0, o]
    order_v[...] = jnp.clip(block, 0, NB - 1)
    order_copy = pltpu.make_async_copy(order_v, order, order_sem)
    order_copy.start()
    pooled_last[...] = jnp.zeros_like(pooled_last)
    for i in (2, 3, 4):
        arg_copies[i].wait()
    for b in range(NB):
        bias2[b] = bias_ref[b * BLOCK : (b + 1) * BLOCK].reshape(1, BLOCK)

    def norm_rows(tok, chunk, at):
        adapted = jnp.dot(tok, aw_ref[...], preferred_element_type=jnp.float32)
        centred = adapted - jnp.mean(adapted, axis=-1, keepdims=True)
        row_var = jnp.mean(centred * centred, axis=-1, keepdims=True)
        normed = centred * lax.rsqrt(row_var + EPSILON) * gain_ref[...].reshape(1, -1)
        hid[chunk, pl.ds(at, tok.shape[0]), :] = normed.astype(jnp.bfloat16)

    def head_step(chunk, i):
        per = TILE // BLOCK
        at = range(i * per, (i + 1) * per)
        if chunk == 3:
            at = [order[0, b] for b in at]
        bias = jnp.concatenate([bias2[b] for b in at], axis=1)
        weights = jnp.concatenate([wbuf[b] for b in at], axis=1)
        logits = jnp.dot(hid[chunk], weights, preferred_element_type=jnp.float32)
        x = jnp.maximum(jnp.max(logits.reshape(4, LEN, TILE), axis=1) + bias, 0.0)
        for _ in range(3):
            x = x * (x + 2.0)
        row = chunk % 2 * 4
        for q in range(per):
            part = x[:, q * BLOCK : (q + 1) * BLOCK]
            if chunk == 3:
                pooled_last[i * per + q, row : row + 4] = part
            else:
                pooled[chunk // 2, i * per + q, row : row + 4] = part

    row8 = lax.broadcasted_iota(jnp.int32, (8, BLOCK), 0)

    def tiles_of(k, o, r):
        at = starts[o]
        two = [pooled[k, at], pooled[k, jnp.minimum(at + 1, NB - 1)]]
        if k == 1:
            at = firsts[r]
            late = [pooled_last[at], pooled_last[jnp.minimum(at + 1, NB - 1)]]
            two = [jnp.where(row8 < 4, a, b) for a, b in zip(two, late)]
        send[k, o] = jnp.concatenate(two, axis=0).astype(jnp.bfloat16)

    def send_tile(k, r):
        o = across(*owners[r])
        tiles_of(k, o, r)
        pltpu.make_async_remote_copy(
            src_ref=send.at[k, o],
            dst_ref=recv_ref.at[k, d],
            send_sem=tile_send.at[k],
            recv_sem=tile_recv.at[k],
            device_id=(o, v),
            device_id_type=MESH,
        ).start()

    def keep_tile(k):
        tiles_of(k, d, OWNERS - 1)
        pltpu.make_async_copy(send.at[k, d], recv_ref.at[k, d], tile_own.at[k]).start()

    def norm_chunk(chunk, buf, piece, pieces):
        rows = CHUNK // pieces
        tok = buf[piece * rows // SHARD, piece * rows % SHARD : piece * rows % SHARD + rows, :]
        norm_rows(tok, chunk, piece * rows)

    for i in range(2):
        norm_rows(tok_own[i * LEN : (i + 1) * LEN], 0, pl.multiple_of(c * SHARD + i * LEN, 16))
    tokens_in(0)
    for r in (5, 6):
        token_copy(r, c).start()
    for i in range(2):
        norm_rows(tok_a[i * LEN : (i + 1) * LEN], 0, pl.multiple_of((1 - c) * SHARD + i * LEN, 16))
    told(0)
    tell(1)
    pltpu.make_async_copy(wbuf, wbuf, wsem).wait()
    for i in range(STEPS - 1):
        head_step(0, i)

    def norm_near(buf, core):
        for i in range(2):
            norm_rows(buf[i * LEN : (i + 1) * LEN], 1, pl.multiple_of(core * SHARD + i * LEN, 16))

    told(1)
    tell(2)
    tokens_in(1)
    head_step(0, STEPS - 1)
    norm_near(tok_b0, c)
    tokens_in(2)
    norm_near(tok_b1, 1 - c)
    tokens_in(3)
    tokens_in(4)
    told(2)
    tell(3)
    for i in range(STEPS):
        head_step(1, i)
        if i < 4:
            norm_chunk(2, tok_c, i, 4)
    tokens_in(5)
    tokens_in(6)
    told(3)
    tell(4)
    for i in range(STEPS):
        head_step(2, i)
        if i < 4:
            norm_chunk(3, tok_d, i, 4)
    told(4)

    order_copy.wait()
    for r in range(OWNERS - 1):
        send_tile(0, r)
    keep_tile(0)
    early = TILE // BLOCK // 2
    for i in range(STEPS):
        head_step(3, i)
        if i == 2:
            for r in range(min(3 * early, OWNERS - 1)):
                send_tile(1, r)
    for r in range(3 * early, OWNERS - 1):
        send_tile(1, r)
    keep_tile(1)

    def tiles_in(k):
        pltpu.make_async_copy(send.at[k, d], recv_ref.at[k, d], tile_own.at[k]).wait()
        others = recv_ref.at[k, 0 : OWNERS - 1]
        pltpu.make_async_copy(others, others, tile_recv.at[k]).wait()

    def codes(k, s):
        return recv_ref[k, :, s * 8 : (s + 1) * 8, :].astype(jnp.float32)

    def in_order(k, rows):
        return jnp.where(y % 2 == 1 - k, jnp.concatenate([rows[:, 4:], rows[:, :4]], axis=1), rows)

    tiles_in(0)
    tops = []
    for s in range(2):
        code = codes(0, s)
        tops.append(jnp.max(code, axis=0))
        impact[s] = in_order(0, jnp.log1p(code))
    for r in range(7):
        token_copy(r, c).wait_send()
    sent = send.at[0, 0 : OWNERS - 1]
    pltpu.make_async_copy(sent, sent, tile_send.at[0]).wait()

    tiles_in(1)
    count = jnp.full((8, BLOCK), counts_ref[0, d])
    for s in range(2):
        code = codes(1, s)
        top = jnp.max(jnp.maximum(tops[s], jnp.max(code, axis=0)), axis=0, keepdims=True)
        factor = 0.125 / jnp.maximum(jnp.log1p(top) * 0.125, 1.0)
        out_ref[s, :, y // 2] = jnp.where(count > s, impact[s] * factor, 0.0)
        out_ref[s, :, 1 - y // 2] = jnp.where(count > s, in_order(1, jnp.log1p(code)) * factor, 0.0)
    sent = send.at[1, 0 : OWNERS - 1]
    pltpu.make_async_copy(sent, sent, tile_send.at[1]).wait()


def shards(tokens, token_mask, adapter_weight, norm_gain, head_weight, head_bias, block_counts):
    hbm = pl.BlockSpec(memory_space=pltpu.HBM)
    scaled = pl.pallas_call(
        index_kernel,
        out_shape=jax.ShapeDtypeStruct((2, OWNERS, 2, 8, BLOCK), jnp.float32),
        in_specs=[hbm] * 7,
        out_specs=pl.BlockSpec(memory_space=pltpu.VMEM),
        scratch_shapes=[
            pltpu.VMEM((2, LEN, BLOCK), jnp.bfloat16),
            pltpu.VMEM((2, LEN), jnp.int32),
            pltpu.VMEM((BLOCK, 768), jnp.bfloat16),
            pltpu.VMEM((768,), jnp.float32),
            pltpu.VMEM((NB * BLOCK,), jnp.float32),
            pltpu.VMEM((NB, 1, BLOCK), jnp.float32),
            pltpu.SMEM((1, OWNERS), jnp.int32),
            pltpu.VMEM((SHARD, BLOCK), jnp.bfloat16),
            pltpu.VMEM((SHARD, BLOCK), jnp.bfloat16),
            pltpu.VMEM((SHARD, BLOCK), jnp.bfloat16),
            pltpu.VMEM((SHARD, BLOCK), jnp.bfloat16),
            pltpu.VMEM((2, SHARD, BLOCK), jnp.bfloat16),
            pltpu.VMEM((2, SHARD, BLOCK), jnp.bfloat16),
            pltpu.VMEM((4, CHUNK, 768), jnp.bfloat16),
            pltpu.VMEM((NB, 768, BLOCK), jnp.bfloat16),
            pltpu.VMEM((2, NB, 8, BLOCK), jnp.float32),
            pltpu.VMEM((NB, 8, BLOCK), jnp.float32),
            pltpu.VMEM((2, OWNERS, 16, BLOCK), jnp.bfloat16),
            pltpu.VMEM((2, OWNERS, 16, BLOCK), jnp.bfloat16),
            pltpu.VMEM((2, OWNERS, 8, BLOCK), jnp.float32),
            pltpu.SMEM((OWNERS,), jnp.int32),
            pltpu.SMEM((OWNERS,), jnp.int32),
            pltpu.VMEM((8, BLOCK), jnp.int32),
            pltpu.SMEM((8, BLOCK), jnp.int32),
            pltpu.SemaphoreType.DMA((6,)),
            pltpu.SemaphoreType.DMA,
            pltpu.SemaphoreType.DMA,
            pltpu.SemaphoreType.DMA((7,)),
            pltpu.SemaphoreType.DMA((7,)),
            pltpu.SemaphoreType.REGULAR((5, 2)),
            pltpu.SemaphoreType.DMA((2,)),
            pltpu.SemaphoreType.DMA((2,)),
            pltpu.SemaphoreType.DMA((2,)),
        ],
        compiler_params=pltpu.CompilerParams(
            collective_id=0, has_side_effects=True, vmem_limit_bytes=48 * 2**20
        ),
        cost_estimate=pl.CostEstimate(
            flops=8_000_000_000, bytes_accessed=7_000_000, transcendentals=0
        ),
        name="index",
    )(*(
        pltpu.with_memory_space_constraint(x, pltpu.HBM)
        for x in (
            tokens, token_mask, adapter_weight, norm_gain, head_bias, block_counts, head_weight
        )
    ))
    return scaled.reshape(2, OWNERS * 16, BLOCK)


def solution(mesh):
    in_specs = (
        P(("docs", "vocab"), None, None),
        P(("docs", "vocab"), None),
        P(),
        P(),
        P(None, "vocab"),
        P("vocab"),
        P("vocab", None),
    )
    out_specs = P("docs", None, "vocab")
    return jax.shard_map(shards, mesh=mesh, in_specs=in_specs, out_specs=out_specs, check_vma=False)
```
